512 devices in a mesh: ctx: 64 (over x, y, core), tp: 8 (over z).
Axes of the slice: x: 4, y: 8, z: 8, core: 2. Of those that a mesh axis runs over, the one named last changes fastest.
Arguments:
- queries: bfloat16 [128, 2, 64, 128], P('ctx', None, 'tp'), may hold values from -64 to 64
- prefix_keys: bfloat16 [131072, 8, 128], P('ctx', 'tp'), may hold values from -8 to 8
- prefix_values: bfloat16 [131072, 8, 128], P('ctx', 'tp'), may hold values from -6 to 6
- suffix_keys: bfloat16 [128, 1024, 8, 128], P('ctx', None, 'tp'), may hold values from -8 to 8
- suffix_values: bfloat16 [128, 1024, 8, 128], P('ctx', None, 'tp'), may hold values from -6 to 6
- new_keys: bfloat16 [128, 2, 8, 128], P('ctx', None, 'tp'), may hold values from -12 to 12
- new_values: bfloat16 [128, 2, 8, 128], P('ctx', None, 'tp'), may hold values from -6 to 6
- suffix_lengths: int32 [128], P('ctx'), may hold values from 1 to 1024, 65536 in all
- out_weight: bfloat16 [8192, 8192], P('tp', 'ctx'), may hold values from -0.0625 to 0.0625
Outputs:
- projected: bfloat16 [128, 2, 8192], P('tp', None, 'ctx')
The draws below stay inside these ranges and needn't reach their ends.
All inputs are finite; a program needn't handle non-finite values. No bound on the sum of `suffix_lengths` on one device may be relied on, other than what follows from the above.
Results may differ from the reference program's by a relative error of at most 0.02.
Values may be sent and summed in bfloat16 or wider, within the bound.
A program may use at most 192 MiB of HBM per device.

```python
import math
import jax
import jax.numpy as jnp
import numpy as np
from jax import lax

D = 8192
HEADS = 64
KV_HEADS = 8
HD = 128
SUF_MAX = 1024
STEPS = 2
PROMPT = 131072
SAMPLES = 128


def draw_queries(key, part):
    key = jax.random.fold_in(key, 11)
    subkeys = jax.random.split(key, 1)
    drawn = 1.5 * jax.random.normal(subkeys[0], (SAMPLES, STEPS, HEADS, HD), jnp.float32)
    return jnp.clip(drawn, -9.0, 9.0).astype(jnp.bfloat16)


def draw_prefix_keys(key, part):
    key = jax.random.fold_in(key, 12)
    subkeys = jax.random.split(key, 1)
    drawn = jax.random.normal(subkeys[0], (PROMPT, KV_HEADS, HD), jnp.float32)
    return jnp.clip(drawn, -6.0, 6.0).astype(jnp.bfloat16)


def levels(rng, shape, cuts, low, top_value):
    def one(position, blocks):
        steps = jax.random.uniform(jax.random.fold_in(jax.random.fold_in(rng, 6), position), (blocks,), jnp.float32, low / len(cuts), top_value / len(cuts))
        return jnp.repeat(jnp.exp(steps), shape[position] // blocks).reshape((-1,) + (1,) * (len(shape) - position - 1))

    loudness = one(*cuts[0])
    for cut in cuts[1:]:
        loudness = loudness * one(*cut)
    return loudness


def profile(count, total, bound, lean):
    weights = [(1 << 20) // math.isqrt(standing ** lean) + 1 for standing in range(2, count + 1)]
    rest, given = total - bound - (count - 1), [1] * (count - 1)
    while rest > 0:
        free = [i for i in range(count - 1) if given[i] < bound]
        pool, left = sum([weights[i] for i in free]), rest
        for i in free:
            addition = min(bound - given[i], max(1, left * weights[i] // pool), rest)
            given[i] = given[i] + addition
            rest = rest - addition
    return np.array([bound] + given)


def ragged_sizes(rng, amount, total, limit, skew):
    if amount == 2:
        one = jax.random.randint(rng, (), max(1, total - limit), min(limit, total - 1) + 1)
        return jnp.stack([one, total - one])
    tallies = jnp.asarray(profile(amount, total, limit, skew), jnp.int32)
    couples = (amount - 1) // 2
    giver, taker = tallies[1:1 + 2 * couples:2], tallies[2:2 + 2 * couples:2]
    slack = jnp.minimum(giver - 1, limit - taker)
    shifted = jax.random.randint(jax.random.fold_in(rng, 1), (couples,), 0, 1 << 20) % (slack + 1)
    tallies = tallies.at[1:1 + 2 * couples:2].set(giver - shifted).at[2:2 + 2 * couples:2].set(taker + shifted)
    return tallies[jax.random.permutation(jax.random.fold_in(rng, 2), amount)]


def normal_values(key, dims, scale, reach, cuts=(), kind=jnp.bfloat16):
    array = scale * jax.random.normal(key, dims, jnp.float32)
    if cuts:
        array = array * levels(key, dims, cuts, -0.22, 0.18)
    return jnp.clip(array, -reach, reach).astype(kind)


def setup_inputs(seed: int = 0) -> dict:
    seeds = jax.random.split(jax.random.key(seed), 10)
    queries = draw_queries(jax.random.fold_in(seeds[9], 71), 0)
    prefix_keys = draw_prefix_keys(jax.random.fold_in(seeds[9], 71), 0)
    prefix_values = normal_values(seeds[2], (PROMPT, KV_HEADS, HD), 1.0, 6.0, ((0, 64), (1, 8)))
    suffix_keys = normal_values(seeds[3], (SAMPLES, SUF_MAX, KV_HEADS, HD), 1.3, 8.0, ((0, 64), (2, 8)))
    suffix_values = normal_values(seeds[4], (SAMPLES, SUF_MAX, KV_HEADS, HD), 1.0, 6.0, ((0, 64), (2, 8)))
    new_keys = normal_values(seeds[5], (SAMPLES, STEPS, KV_HEADS, HD), 2.0, 12.0, ((0, 64), (2, 8)))
    new_values = normal_values(seeds[6], (SAMPLES, STEPS, KV_HEADS, HD), 1.0, 6.0, ((0, 64), (2, 8)))
    suffix_lengths = ragged_sizes(seeds[7], SAMPLES, SAMPLES * SUF_MAX // 2, SUF_MAX, 1).astype(jnp.int32)
    out_weight = normal_values(seeds[8], (HEADS * HD, D), (HEADS * HD) ** -0.5, 0.0625, ((0, 8), (1, 64)))
    return dict(queries=queries, prefix_keys=prefix_keys, prefix_values=prefix_values, suffix_keys=suffix_keys, suffix_values=suffix_values, new_keys=new_keys, new_values=new_values, suffix_lengths=suffix_lengths, out_weight=out_weight)


masked_score = -1.0e30


def rounded_weights(weights):
    return lax.optimization_barrier(weights.astype(jnp.bfloat16)).astype(jnp.float32)


def reference(queries, prefix_keys, prefix_values, suffix_keys, suffix_values, new_keys, new_values, suffix_lengths, out_weight):
    group_size = HEADS // KV_HEADS
    score_scale = HD ** -0.5
    block_width = math.gcd(SAMPLES, 8)
    blocks = SAMPLES // block_width
    query_blocks = queries.reshape(blocks, block_width, STEPS, KV_HEADS, group_size, HD)
    suffix_key_blocks = suffix_keys.reshape(blocks, block_width, SUF_MAX, KV_HEADS, HD)
    suffix_value_blocks = suffix_values.reshape(blocks, block_width, SUF_MAX, KV_HEADS, HD)
    new_key_blocks = new_keys.reshape(blocks, block_width, STEPS, KV_HEADS, HD)
    new_value_blocks = new_values.reshape(blocks, block_width, STEPS, KV_HEADS, HD)
    length_blocks = suffix_lengths.reshape(blocks, block_width)
    prompt_keys = jnp.transpose(prefix_keys, (1, 0, 2))
    prompt_values = jnp.transpose(prefix_values, (1, 0, 2))
    causal = (jnp.arange(STEPS, dtype=jnp.int32)[:, None] >= jnp.arange(STEPS, dtype=jnp.int32)[None, :])[None, :, None, :]

    def attend_block(pieces):
        query_block, suffix_key_block, suffix_value_block, new_key_block, new_value_block, length_block = pieces
        live_slots = (jnp.arange(SUF_MAX, dtype=jnp.int32)[None, :] < length_block[:, None])[:, None, None, :]

        def attend_head(head_pieces):
            query_head, prompt_key, prompt_value, suffix_key, suffix_value, new_key, new_value = head_pieces
            query_float = query_head.astype(jnp.float32)
            prefix_scores = jnp.einsum("stgd,jd->stgj", query_float, prompt_key.astype(jnp.float32)) * score_scale
            suffix_scores = jnp.einsum("stgd,sjd->stgj", query_float, suffix_key.astype(jnp.float32)) * score_scale
            suffix_scores = jnp.where(live_slots, suffix_scores, masked_score)
            recent_scores = jnp.einsum("stgd,sud->stgu", query_float, new_key.astype(jnp.float32)) * score_scale
            recent_scores = jnp.where(causal, recent_scores, masked_score)
            row_top = jnp.maximum(jnp.max(prefix_scores, axis=-1), jnp.maximum(jnp.max(suffix_scores, axis=-1), jnp.max(recent_scores, axis=-1)))
            prefix_weights = jnp.exp(prefix_scores - row_top[..., None])
            suffix_weights = jnp.where(live_slots, jnp.exp(suffix_scores - row_top[..., None]), 0.0)
            recent_weights = jnp.where(causal, jnp.exp(recent_scores - row_top[..., None]), 0.0)
            row_total = jnp.sum(prefix_weights, axis=-1) + jnp.sum(suffix_weights, axis=-1) + jnp.sum(recent_weights, axis=-1)
            weighted = jnp.einsum("stgj,jd->stgd", rounded_weights(prefix_weights), prompt_value.astype(jnp.float32))
            weighted = weighted + jnp.einsum("stgj,sjd->stgd", rounded_weights(suffix_weights), suffix_value.astype(jnp.float32))
            weighted = weighted + jnp.einsum("stgu,sud->stgd", rounded_weights(recent_weights), new_value.astype(jnp.float32))
            return (weighted / row_total[..., None]).astype(jnp.bfloat16)

        per_head = lax.map(attend_head, (
            jnp.transpose(query_block, (2, 0, 1, 3, 4)),
            prompt_keys,
            prompt_values,
            jnp.transpose(suffix_key_block, (2, 0, 1, 3)),
            jnp.transpose(suffix_value_block, (2, 0, 1, 3)),
            jnp.transpose(new_key_block, (2, 0, 1, 3)),
            jnp.transpose(new_value_block, (2, 0, 1, 3)),
        ))
        return jnp.transpose(per_head, (1, 2, 0, 3, 4)).reshape(block_width, STEPS, HEADS * HD)

    attention = lax.map(attend_block, (query_blocks, suffix_key_blocks, suffix_value_blocks, new_key_blocks, new_value_blocks, length_blocks))
    attention = attention.reshape(SAMPLES * STEPS, HEADS * HD)
    projected = jnp.dot(attention, out_weight, preferred_element_type=jnp.float32).astype(jnp.bfloat16)
    return projected.reshape(SAMPLES, STEPS, D)
```

```python
import functools
import math

import jax
import jax.numpy as jnp
from jax import lax
from jax.experimental import pallas as pl
from jax.experimental.pallas import tpu as pltpu
from jax.sharding import PartitionSpec as P

MESH = pl.DeviceIdType.MESH
LANES = 128
CORES = 2
masked_score = -1e30


def dot_rows(left, right):
    return lax.dot_general(
        left, right, (((1,), (1,)), ((), ())), preferred_element_type=jnp.float32
    )


def attend_kernel(
    sizes,
    q_ref,
    k_ref,
    v_ref,
    sk_ref,
    sv_ref,
    nk_ref,
    nv_ref,
    len_ref,
    w_ref,
    out_ref,
    kbuf,
    vbuf,
    skbuf,
    svbuf,
    nkbuf,
    nvbuf,
    wbuf,
    qbuf,
    parts,
    part_tops,
    sib_parts,
    sib_tops,
    merged,
    merged_tops,
    x_parts,
    x_tops,
    y_send,
    y_send_tops,
    y_parts,
    y_tops,
    suffix_part,
    suffix_top,
    abuf,
    attention32,
    z_send,
    z_parts,
    local_sem,
    send_sem,
    recv_sem,
    z_send_sem,
    z_recv_sem,
):
    nx, ny, nz = sizes
    rows = q_ref.shape[0]
    chunk = ny * rows
    stat_rows = chunk // LANES
    groups = LANES // rows
    head_dim = q_ref.shape[1]
    samp_dev, slots = sk_ref.shape[0], sk_ref.shape[1]
    samp_rows = rows // samp_dev
    steps = nk_ref.shape[1]
    heads = samp_rows // steps
    log2_scale = (head_dim ** (-0.5)) * math.log2(math.e)

    me = lax.axis_index("ctx")
    z0 = lax.axis_index("tp")
    c0 = lax.rem(me, CORES)
    y0 = lax.rem(lax.div(me, CORES), ny)
    x0 = lax.div(me, CORES * ny)

    def at(x, y, c):
        return {"ctx": (x * ny + y) * CORES + c}

    def x_plus(d):
        return lax.rem(x0 + d, nx)

    def y_plus(d):
        return lax.rem(y0 + d, ny)

    sibling = at(x0, y0, 1 - c0)
    cother = 1 - c0

    bases = {}
    count = 0
    for name, amount in (
        ("qy", ny),
        ("qx", nx),
        ("qc", nx),
        ("pc", nx),
        ("pct", nx),
        ("px", nx),
        ("pxt", nx),
        ("py", ny),
        ("pyt", ny),
        ("ay", ny),
        ("ax", nx),
        ("ac", nx),
    ):
        bases[name] = count
        count += amount

    def remote(name, d, src, dst, device):
        slot = bases[name] + d
        return pltpu.make_async_remote_copy(
            src_ref=src,
            dst_ref=dst,
            send_sem=send_sem.at[slot],
            recv_sem=recv_sem.at[slot],
            device_id=device,
            device_id_type=MESH,
        )

    def q_y(d):
        return remote("qy", d, q_ref, qbuf.at[x0, c0, y0], at(x0, y_plus(d), c0))

    def q_x(d):
        return remote("qx", d, qbuf.at[x0, c0], qbuf.at[x0, c0], at(x_plus(d), y0, c0))

    def q_core(dx):
        x = x_plus(dx)
        return remote("qc", dx, qbuf.at[x, c0], qbuf.at[x, c0], sibling)

    def p_core(dx):
        return remote("pc", dx, parts.at[1, dx], sib_parts.at[dx], sibling)

    def pt_core(dx):
        return remote("pct", dx, part_tops.at[1, dx], sib_tops.at[dx], sibling)

    def p_x(dx):
        return remote("px", dx, merged.at[dx], x_parts.at[dx], at(x_plus(dx), y0, c0))

    def pt_x(dx):
        return remote("pxt", dx, merged_tops.at[dx], x_tops.at[dx], at(x_plus(dx), y0, c0))

    def p_y(d):
        y = y_plus(d)
        return remote("py", d, y_send.at[y], y_parts.at[y0], at(x0, y, c0))

    def pt_y(d):
        y = y_plus(d)
        return remote(
            "pyt",
            d,
            y_send_tops.at[(-d) % groups, lax.div(y, groups)],
            y_tops.at[y0],
            at(x0, y, c0),
        )

    def a_y(d):
        mine = abuf.at[x0, y0, c0]
        return remote("ay", d, mine, mine, at(x0, y_plus(d), c0))

    def a_x(d):
        mine = abuf.at[x0, :, c0]
        return remote("ax", d, mine, mine, at(x_plus(d), y0, c0))

    def a_core(dx):
        mine = abuf.at[x_plus(dx), :, c0]
        return remote("ac", dx, mine, mine, sibling)

    def z_copy(dx, j):
        z = x_plus(dx) * (nz // nx) + j
        d = lax.rem(z - z0 + nz, nz)
        return z, pltpu.make_async_remote_copy(
            src_ref=z_send.at[dx, j],
            dst_ref=z_parts.at[z0],
            send_sem=z_send_sem.at[dx, j],
            recv_sem=z_recv_sem.at[d],
            device_id={"tp": z},
            device_id_type=MESH,
        )

    barrier = pltpu.get_barrier_semaphore()
    partners = [at(x0, y_plus(d), c0) for d in range(1, ny)]
    partners += [at(x_plus(d), y0, c0) for d in range(1, nx)]
    partners += [sibling]
    partners += [{"tp": lax.rem(z0 + d, nz)} for d in range(1, nz)]
    for partner in partners:
        pl.semaphore_signal(barrier, inc=1, device_id=partner, device_id_type=MESH)

    local = [
        pltpu.make_async_copy(q_ref, qbuf.at[x0, c0, y0], local_sem.at[0]),
        pltpu.make_async_copy(sk_ref, skbuf, local_sem.at[1]),
        pltpu.make_async_copy(nk_ref, nkbuf, local_sem.at[2]),
        pltpu.make_async_copy(nv_ref, nvbuf, local_sem.at[3]),
        pltpu.make_async_copy(sv_ref, svbuf, local_sem.at[4]),
        pltpu.make_async_copy(k_ref, kbuf, local_sem.at[5]),
        pltpu.make_async_copy(v_ref, vbuf.at[:, 0:head_dim], local_sem.at[6]),
        pltpu.make_async_copy(w_ref, wbuf, local_sem.at[7]),
    ]
    for copy in local:
        copy.start()
    vbuf[:, head_dim:] = jnp.ones((vbuf.shape[0], LANES), jnp.bfloat16)

    pl.semaphore_wait(barrier, len(partners))
    order = sorted(range(1, ny), key=lambda d: -min(d, ny - d))
    for d in order:
        q_y(d).start()

    for copy in local[:5]:
        copy.wait()
    own_queries = qbuf[x0, c0, y0]
    row_in_sample = lax.broadcasted_iota(jnp.int32, (samp_rows, 1), 0)
    slot_index = lax.broadcasted_iota(jnp.int32, (samp_rows, slots), 1)
    outs, tops = [], []
    for s in range(samp_dev):
        queries = own_queries[s * samp_rows : (s + 1) * samp_rows]
        scores = dot_rows(queries, skbuf[s])
        scores = jnp.where(slot_index < len_ref[s], scores, masked_score)
        new_keys = nkbuf[s].astype(jnp.float32)
        new_values = nvbuf[s].astype(jnp.float32)
        row_top = jnp.max(scores, axis=1, keepdims=True)
        recent = []
        for u in range(steps):
            score = jnp.sum(
                queries.astype(jnp.float32) * new_keys[u : u + 1], axis=1, keepdims=True
            )
            score = jnp.where(row_in_sample >= u * heads, score, masked_score)
            row_top = jnp.maximum(row_top, score)
            recent.append(score)
        weights = jnp.exp2((scores - row_top) * log2_scale)
        row_total = jnp.sum(weights, axis=1, keepdims=True)
        weighted = jnp.dot(
            weights.astype(jnp.bfloat16), svbuf[s], preferred_element_type=jnp.float32
        )
        for u in range(steps):
            weight = jnp.exp2((recent[u] - row_top) * log2_scale)
            row_total = row_total + weight
            weighted = weighted + weight.astype(jnp.bfloat16).astype(jnp.float32) * (
                new_values[u : u + 1]
            )
        suffix_part[s * samp_rows : (s + 1) * samp_rows, :] = weighted / row_total
        outs.append(row_top * log2_scale + jnp.log2(row_total))
    lane = lax.broadcasted_iota(jnp.int32, (rows, LANES), 1)
    sub = lax.broadcasted_iota(jnp.int32, (rows, LANES), 0)
    suffix_top[...] = jnp.sum(
        jnp.where(lax.rem(lane, rows) == sub, jnp.concatenate(outs, axis=0), 0.0),
        axis=0,
        keepdims=True,
    )

    for d in range(1, ny):
        q_y(d).wait_recv()
    q_core(0).start()
    for d in range(1, nx):
        q_x(d).start()
    local[5].wait()
    local[6].wait()

    eye = lax.broadcasted_iota(jnp.int32, (LANES, LANES), 0) == lax.broadcasted_iota(
        jnp.int32, (LANES, LANES), 1
    )

    def attend(queries):
        scores = dot_rows(queries, kbuf[...])
        row_top = jnp.max(scores, axis=1, keepdims=True)
        weights = jnp.exp2((scores - row_top) * log2_scale).astype(jnp.bfloat16)
        both = jnp.dot(weights, vbuf[...], preferred_element_type=jnp.float32)
        total = both[:, head_dim:]
        part = (both[:, :head_dim] / total).astype(jnp.bfloat16)
        return part, row_top * log2_scale + jnp.log2(total)

    def combine(sources):
        top = sources[0][1]
        for _, stat in sources[1:]:
            top = jnp.maximum(top, stat)
        weights = [jnp.exp2(stat - top) for _, stat in sources]
        total = sum(weights[1:], weights[0])
        inverse = 1.0 / total
        joined_top = top + jnp.log2(total)
        joined = []
        for g in range(stat_rows):
            result = None
            for (read, _), weight in zip(sources, weights):
                spread = jnp.where(eye, (weight * inverse)[g : g + 1], 0.0)
                term = jnp.dot(
                    spread.astype(jnp.bfloat16), read(g), preferred_element_type=jnp.float32
                )
                result = term if result is None else result + term
            joined.append(result.astype(jnp.bfloat16))
        return joined, joined_top

    def reader(ref, *index):
        return lambda g: ref[(*index, pl.ds(g * LANES, LANES))]

    def stats(ref, *index):
        return ref[index][0:stat_rows]

    def merge_pair(dx):
        p_core(dx).wait_recv()
        pt_core(dx).wait_recv()
        joined, top = combine(
            [
                (reader(parts, 0, dx), stats(part_tops, 0, dx)),
                (reader(sib_parts, dx), stats(sib_tops, dx)),
            ]
        )
        for g in range(stat_rows):
            merged[dx, pl.ds(g * LANES, LANES)] = joined[g]
        merged_tops[dx, 0:stat_rows] = top
        p_x(dx).start()
        pt_x(dx).start()

    last = 2 * nx - 1

    def step(i, carry):
        dx = lax.rem(lax.div(i + 1, 2), nx)
        flag = lax.rem(i, 2) + lax.div(last - i, last) - lax.div(i, last)
        for k in range(1, nx):

            @pl.when(i == 2 * k - 1)
            def _():
                for ahead in range(1, nx) if k == 1 else ():
                    q_x(nx - ahead).wait_recv()
                    q_core(ahead).start()
                q_core(k).wait_recv()

        @pl.when(i == 0)
        def _():
            q_core(0).wait_recv()

        queries = qbuf[x_plus(dx), lax.rem(c0 + flag, CORES)].reshape(chunk, head_dim)
        part, top = attend(queries)
        parts[flag, dx] = part
        for g in range(stat_rows):
            part_tops[flag, dx, g : g + 1] = jnp.sum(
                jnp.where(eye, top[g * LANES : (g + 1) * LANES], 0.0), axis=0, keepdims=True
            )

        for k in range(nx):

            @pl.when(i == max(2 * k - 1, 0))
            def _():
                p_core(k).start()
                pt_core(k).start()

        for k in range(1, nx):

            @pl.when(i == 2 * k)
            def _():
                merge_pair(k)

        return carry

    part_tops[...] = jnp.zeros_like(part_tops)
    merged_tops[...] = jnp.zeros_like(merged_tops)
    lax.fori_loop(0, 2 * nx, step, 0)

    p_core(0).wait_recv()
    pt_core(0).wait_recv()
    sources = [
        (reader(parts, 0, 0), stats(part_tops, 0, 0)),
        (reader(sib_parts, 0), stats(sib_tops, 0)),
    ]
    for d in range(1, nx):
        p_x(d).wait_recv()
        pt_x(d).wait_recv()
        sources.append((reader(x_parts, d), stats(x_tops, d)))
    joined, top = combine(sources)
    per_group = LANES // rows
    for g in range(stat_rows):
        for j in range(per_group):
            y_send[g * per_group + j] = joined[g][j * rows : (j + 1) * rows]
    for turn in range(groups):
        turned = pltpu.roll(top, turn * rows, 1) if turn else top
        for g in range(stat_rows):
            y_send_tops[turn, g] = turned[g : g + 1]
    for d in order:
        p_y(d).start()
        pt_y(d).start()
    y_parts[y0] = y_send[y0]
    y_tops[y0] = y_send_tops[0, lax.div(y0, groups)]
    for d in range(1, ny):
        p_y(d).wait_recv()
        pt_y(d).wait_recv()

    lane_row = lax.broadcasted_iota(jnp.int32, (1, LANES), 1)
    flat = []
    for g in range(stat_rows):
        line = jnp.zeros((1, LANES), jnp.float32)
        for j in range(groups):
            line = jnp.where(lax.div(lane_row, rows) == j, y_tops[g * groups + j], line)
        flat.append(line)

    def over_groups(lines, op):
        result = functools.reduce(op, lines)
        turn = LANES // 2
        while turn >= rows:
            result = op(result, pltpu.roll(result, turn, 1))
            turn //= 2
        return result

    own_top = suffix_top[...]
    row_top = jnp.maximum(over_groups(flat, jnp.maximum), own_top)
    flat = [jnp.exp2(line - row_top) for line in flat]
    own_weight = jnp.exp2(own_top - row_top)
    inverse = 1.0 / (over_groups(flat, jnp.add) + own_weight)
    own_column = jnp.sum(
        jnp.where(lane == sub, own_weight * inverse, 0.0), axis=1, keepdims=True
    )
    result = own_column * suffix_part[...]
    for g in range(stat_rows):
        spread = jnp.where(lax.rem(lane, rows) == sub, flat[g] * inverse, 0.0)
        result = result + jnp.dot(
            spread.astype(jnp.bfloat16),
            y_parts[g * groups : (g + 1) * groups].reshape(LANES, head_dim),
            preferred_element_type=jnp.float32,
        )
    abuf[x0, y0, c0] = result.astype(jnp.bfloat16)

    for d in order:
        a_y(d).start()
    for d in range(1, ny):
        a_y(d).wait_recv()
    for d in range(1, nx):
        a_x(d).start()
    a_core(0).start()
    local[7].wait()

    tokens = chunk * CORES // heads
    share = tokens * nx // nz

    def project(dx):
        a_core(dx).wait_recv()
        attention32[...] = (
            abuf[x_plus(dx)].reshape(chunk * CORES, head_dim).astype(jnp.float32)
        )
        features = jnp.concatenate(
            [
                attention32[pl.ds(h, tokens, stride=heads), :].astype(jnp.bfloat16)
                for h in range(heads)
            ],
            axis=1,
        )
        terms = jnp.dot(features, wbuf[...], preferred_element_type=jnp.float32)
        terms = terms.astype(jnp.bfloat16)
        for j in range(nz // nx):
            z_send[dx, j] = terms[j * share : (j + 1) * share]
            z, copy = z_copy(dx, j)

            @pl.when(z != z0)
            def _():
                copy.start()

            @pl.when(z == z0)
            def _():
                z_parts[z0] = z_send[dx, j]

    project(0)
    for dx in range(1, nx):
        a_x(nx - dx).wait_recv()
        a_core(dx).start()
    for dx in range(1, nx):
        project(dx)

    for d in range(1, nz):
        pltpu.make_async_remote_copy(
            src_ref=z_send.at[0, 0],
            dst_ref=z_parts.at[0],
            send_sem=z_send_sem.at[0, 0],
            recv_sem=z_recv_sem.at[d],
            device_id={"tp": z0},
            device_id_type=MESH,
        ).wait_recv()
    total = z_parts[0].astype(jnp.float32)
    for z in range(1, nz):
        total = total + z_parts[z].astype(jnp.float32)
    out_ref[...] = total.astype(jnp.bfloat16)

    for d in range(1, ny):
        for copy in (q_y, p_y, pt_y, a_y):
            copy(d).wait_send()
    for d in range(1, nx):
        for copy in (q_x, p_x, pt_x, a_x):
            copy(d).wait_send()
    for dx in range(nx):
        for copy in (q_core, p_core, pt_core, a_core):
            copy(dx).wait_send()
        for j in range(nz // nx):
            z, copy = z_copy(dx, j)

            @pl.when(z != z0)
            def _():
                copy.wait_send()


def per_device(
    sizes,
    queries,
    prefix_keys,
    prefix_values,
    suffix_keys,
    suffix_values,
    new_keys,
    new_values,
    suffix_lengths,
    out_weight,
):
    nx, ny, nz = sizes
    samp_dev, steps, heads, head_dim = queries.shape
    rows = samp_dev * steps * heads
    chunk = ny * rows
    keys = prefix_keys.shape[0]
    slots = suffix_keys.shape[1]
    columns = out_weight.shape[1]
    tokens = chunk * CORES // heads
    share = tokens * nx // nz
    groups = LANES // rows
    stat_rows = chunk // LANES
    bf16, f32 = jnp.bfloat16, jnp.float32
    sems = 5 * ny + 7 * nx
    anywhere = pl.BlockSpec(memory_space=pl.ANY)
    out = pl.pallas_call(
        functools.partial(attend_kernel, sizes),
        out_shape=jax.ShapeDtypeStruct((share, columns), bf16),
        in_specs=[anywhere] * 7 + [pl.BlockSpec(memory_space=pltpu.SMEM), anywhere],
        out_specs=pl.BlockSpec(memory_space=pltpu.VMEM),
        scratch_shapes=[
            pltpu.VMEM((keys, head_dim), bf16),
            pltpu.VMEM((keys, head_dim + LANES), bf16),
            pltpu.VMEM((samp_dev, slots, head_dim), bf16),
            pltpu.VMEM((samp_dev, slots, head_dim), bf16),
            pltpu.VMEM((samp_dev, steps, head_dim), bf16),
            pltpu.VMEM((samp_dev, steps, head_dim), bf16),
            pltpu.VMEM((heads * head_dim, columns), bf16),
            pltpu.VMEM((nx, CORES, ny, rows, head_dim), bf16),
            pltpu.VMEM((2, nx, chunk, head_dim), bf16),
            pltpu.VMEM((2, nx, 8, LANES), f32),
            pltpu.VMEM((nx, chunk, head_dim), bf16),
            pltpu.VMEM((nx, 8, LANES), f32),
            pltpu.VMEM((nx, chunk, head_dim), bf16),
            pltpu.VMEM((nx, 8, LANES), f32),
            pltpu.VMEM((nx, chunk, head_dim), bf16),
            pltpu.VMEM((nx, 8, LANES), f32),
            pltpu.VMEM((ny, rows, head_dim), bf16),
            pltpu.VMEM((groups, stat_rows, 1, LANES), f32),
            pltpu.VMEM((ny, rows, head_dim), bf16),
            pltpu.VMEM((ny, 1, LANES), f32),
            pltpu.VMEM((rows, head_dim), f32),
            pltpu.VMEM((1, LANES), f32),
            pltpu.VMEM((nx, ny, CORES, rows, head_dim), bf16),
            pltpu.VMEM((chunk * CORES, head_dim), f32),
            pltpu.VMEM((nx, nz // nx, share, columns), bf16),
            pltpu.VMEM((nz, share, columns), bf16),
            pltpu.SemaphoreType.DMA((8,)),
            pltpu.SemaphoreType.DMA((sems,)),
            pltpu.SemaphoreType.DMA((sems,)),
            pltpu.SemaphoreType.DMA((nx, nz // nx)),
            pltpu.SemaphoreType.DMA((nz,)),
        ],
        compiler_params=pltpu.CompilerParams(
            collective_id=0, has_side_effects=True, vmem_limit_bytes=40 * 1024 * 1024
        ),
    )(
        queries.reshape(rows, head_dim),
        prefix_keys.reshape(keys, head_dim),
        prefix_values.reshape(keys, head_dim),
        suffix_keys.reshape(samp_dev, slots, head_dim),
        suffix_values.reshape(samp_dev, slots, head_dim),
        new_keys.reshape(samp_dev, steps, head_dim),
        new_values.reshape(samp_dev, steps, head_dim),
        suffix_lengths,
        out_weight,
    )
    return out.reshape(share // steps, steps, columns)


def solution(mesh, sizes=(4, 8, 8)):
    placed = (
        P("ctx", None, "tp", None),
        P("ctx", "tp", None),
        P("ctx", "tp", None),
        P("ctx", None, "tp", None),
        P("ctx", None, "tp", None),
        P("ctx", None, "tp", None),
        P("ctx", None, "tp", None),
        P("ctx"),
        P("tp", "ctx"),
    )
    return jax.shard_map(
        functools.partial(per_device, sizes),
        mesh=mesh,
        in_specs=placed,
        out_specs=P("tp", None, "ctx"),
        check_vma=False,
    )
```

```python
import functools
import math

import jax
import jax.numpy as jnp
from jax import lax
from jax.experimental import pallas as pl
from jax.experimental.pallas import tpu as pltpu
from jax.sharding import PartitionSpec as P

MESH = pl.DeviceIdType.MESH
LANES = 128
CORES = 2
masked_score = -1e30


def dot_rows(left, right):
    return lax.dot_general(
        left, right, (((1,), (1,)), ((), ())), preferred_element_type=jnp.float32
    )


def dot(left, right):
    return jnp.dot(left, right, preferred_element_type=jnp.float32)


def attend_kernel(
    sizes,
    q_ref,
    k_ref,
    v_ref,
    sk_ref,
    sv_ref,
    nk_ref,
    nv_ref,
    len_ref,
    w_ref,
    out_ref,
    kbuf,
    vbuf,
    skbuf,
    svbuf,
    nkbuf,
    nvbuf,
    wbuf,
    qbuf,
    parts,
    part_tops,
    y_parts,
    y_tops,
    merged,
    merged_top,
    x_parts,
    x_tops,
    suffix_part,
    suffix_top,
    abuf,
    attention32,
    z_send,
    z_parts,
    local_sem,
    send_sem,
    recv_sem,
    qy_sem,
):
    nx, ny, nz = sizes
    rows, head_dim = q_ref.shape
    samp_dev, slots = sk_ref.shape[0], sk_ref.shape[1]
    keys = k_ref.shape[0]
    samp_rows = rows // samp_dev
    steps = nk_ref.shape[1]
    heads = samp_rows // steps
    tokens = rows // heads
    line = nx * rows
    log2_scale = (head_dim ** (-0.5)) * math.log2(math.e)

    me = lax.axis_index("ctx")
    z0 = lax.axis_index("tp")
    c0 = lax.rem(me, CORES)
    y0 = lax.rem(lax.div(me, CORES), ny)
    x0 = lax.div(me, CORES * ny)

    def at(x, y, c):
        return {"ctx": (x * ny + y) * CORES + c}

    def x_peer(d):
        return at(lax.rem(x0 + d + nx, nx), y0, c0)

    def y_peer(d):
        return at(x0, lax.rem(y0 + d + ny, ny), c0)

    sibling = at(x0, y0, 1 - c0)
    z_same = lax.axis_index("ctx")
    z_cross = (x0 * ny + y0) * CORES + 1 - c0

    def remote(src, dst, send, recv, device):
        return pltpu.make_async_remote_copy(
            src_ref=src,
            dst_ref=dst,
            send_sem=send,
            recv_sem=recv,
            device_id=device,
            device_id_type=MESH,
        )

    def family(number):
        return send_sem.at[number], recv_sem.at[number]

    def q_x(d):
        return remote(q_ref, qbuf.at[0, d], *family(0), x_peer(d))

    def q_y(d):
        return remote(qbuf.at[0], qbuf.at[d], send_sem.at[1], qy_sem.at[d], y_peer(d))

    def k_core():
        return remote(k_ref, kbuf.at[1], *family(2), sibling)

    def v_core():
        return remote(v_ref, vbuf.at[1, :, 0:head_dim], *family(3), sibling)

    def w_core():
        return remote(w_ref, wbuf.at[1], *family(4), sibling)

    def p_y(d):
        return remote(parts.at[d], y_parts.at[d], *family(5), y_peer(-d))

    def pt_y(d):
        return remote(part_tops.at[d], y_tops.at[d], *family(6), y_peer(-d))

    def p_x(d):
        return remote(merged.at[d], x_parts.at[d], *family(7), x_peer(-d))

    def pt_x(d):
        return remote(merged_top, x_tops.at[d], *family(8), x_peer(-d))

    def a_y(d):
        return remote(abuf.at[0, 0], abuf.at[0, d], *family(9), y_peer(d))

    def a_x(d):
        return remote(abuf.at[0], abuf.at[d], send_sem.at[10], recv_sem.at[11 + d], x_peer(d))

    def z_copy(dx, j, cross):
        z = lax.rem(x0 - dx + nx, nx) * (nz // nx) + j
        return z, remote(
            z_send.at[dx, j, cross],
            z_parts.at[z0 * CORES + c0],
            *family(11),
            {"ctx": z_cross if cross else z_same, "tp": z},
        )

    barrier = pltpu.get_barrier_semaphore()
    order = sorted(range(1, ny), key=lambda d: -min(d, ny - d))
    partners = [y_peer(d) for d in order] + [x_peer(d) for d in range(1, nx)] + [sibling]
    for d in sorted(range(1, nz), key=lambda d: -min(d, nz - d)):
        z = lax.rem(z0 + d, nz)
        partners += [{"ctx": z_same, "tp": z}, {"ctx": z_cross, "tp": z}]
    for partner in partners:
        pl.semaphore_signal(barrier, inc=1, device_id=partner, device_id_type=MESH)

    local = [
        pltpu.make_async_copy(q_ref, qbuf.at[0, 0], local_sem.at[0]),
        pltpu.make_async_copy(sk_ref, skbuf, local_sem.at[1]),
        pltpu.make_async_copy(nk_ref, nkbuf, local_sem.at[2]),
        pltpu.make_async_copy(nv_ref, nvbuf, local_sem.at[3]),
        pltpu.make_async_copy(sv_ref, svbuf, local_sem.at[4]),
        pltpu.make_async_copy(k_ref, kbuf.at[0], local_sem.at[5]),
        pltpu.make_async_copy(v_ref, vbuf.at[0, :, 0:head_dim], local_sem.at[6]),
        pltpu.make_async_copy(w_ref, wbuf.at[0], local_sem.at[7]),
    ]
    for copy in local:
        copy.start()
    for c in range(CORES):
        vbuf[c, :, head_dim:] = jnp.ones((keys, LANES), jnp.bfloat16)

    pl.semaphore_wait(barrier, len(partners))
    for d in range(1, nx):
        q_x(d).start()
    k_core().start()
    v_core().start()

    for copy in local[:5]:
        copy.wait()
    own_queries = qbuf[0, 0]
    row_in_sample = lax.broadcasted_iota(jnp.int32, (samp_rows, 1), 0)
    slot_index = lax.broadcasted_iota(jnp.int32, (samp_rows, slots), 1)
    tops = []
    for s in range(samp_dev):
        queries = own_queries[s * samp_rows : (s + 1) * samp_rows]
        scores = dot_rows(queries, skbuf[s])
        scores = jnp.where(slot_index < len_ref[s], scores, masked_score)
        new_keys = nkbuf[s].astype(jnp.float32)
        new_values = nvbuf[s].astype(jnp.float32)
        row_top = jnp.max(scores, axis=1, keepdims=True)
        recent = []
        for u in range(steps):
            score = jnp.sum(
                queries.astype(jnp.float32) * new_keys[u : u + 1], axis=1, keepdims=True
            )
            score = jnp.where(row_in_sample >= u * heads, score, masked_score)
            row_top = jnp.maximum(row_top, score)
            recent.append(score)
        weights = jnp.exp2((scores - row_top) * log2_scale)
        row_total = jnp.sum(weights, axis=1, keepdims=True)
        weighted = dot(weights.astype(jnp.bfloat16), svbuf[s])
        for u in range(steps):
            weight = jnp.exp2((recent[u] - row_top) * log2_scale)
            row_total = row_total + weight
            weighted = weighted + weight.astype(jnp.bfloat16).astype(jnp.float32) * (
                new_values[u : u + 1]
            )
        suffix_part[s * samp_rows : (s + 1) * samp_rows, :] = weighted / row_total
        tops.append(row_top * log2_scale + jnp.log2(row_total))
    lane = lax.broadcasted_iota(jnp.int32, (rows, LANES), 1)
    sub = lax.broadcasted_iota(jnp.int32, (rows, LANES), 0)
    suffix_top[...] = jnp.sum(
        jnp.where(lax.rem(lane, rows) == sub, jnp.concatenate(tops, axis=0), 0.0),
        axis=0,
        keepdims=True,
    )

    remote(qbuf.at[0, 1:nx], qbuf.at[0, 1:nx], *family(0), sibling).wait_recv()
    for d in range(1, ny):
        q_y(d).start()
    local[5].wait()
    local[6].wait()
    k_core().wait_recv()
    v_core().wait_recv()
    w_core().start()

    eye = lax.broadcasted_iota(jnp.int32, (LANES, LANES), 0) == lax.broadcasted_iota(
        jnp.int32, (LANES, LANES), 1
    )
    width = min(keys, 256)

    def attend(queries):
        row_top = weighted = None
        for c in range(CORES):
            for start in range(0, keys, width):
                scores = dot_rows(queries, kbuf[c, start : start + width])
                block_top = jnp.max(scores, axis=1, keepdims=True)
                top = block_top if row_top is None else jnp.maximum(row_top, block_top)
                weights = jnp.exp2((scores - top) * log2_scale).astype(jnp.bfloat16)
                term = dot(weights, vbuf[c, start : start + width])
                if row_top is not None:
                    term = weighted * jnp.exp2((row_top - top) * log2_scale) + term
                row_top, weighted = top, term
        total = weighted[:, head_dim:]
        part = (weighted[:, :head_dim] / total).astype(jnp.bfloat16)
        return part, row_top * log2_scale + jnp.log2(total)

    def pair(k, carry):
        first, second = 2 * k + 1, lax.rem(2 * k + 2, ny)
        q_y(first).wait_recv()

        @pl.when(second != 0)
        def _():
            q_y(second).wait_recv()

        queries = jnp.concatenate(
            [qbuf[first].reshape(line, head_dim), qbuf[second].reshape(line, head_dim)], axis=0
        )
        part, top = attend(queries)
        for i, slot in enumerate((first, second)):
            parts[slot] = part[i * line : (i + 1) * line].reshape(nx, rows, head_dim)
            part_tops[slot] = jnp.sum(
                jnp.where(eye, top[i * line : (i + 1) * line], 0.0), axis=0, keepdims=True
            )
        p_y(first).start()
        pt_y(first).start()

        @pl.when(second != 0)
        def _():
            p_y(second).start()
            pt_y(second).start()

        return carry

    lax.fori_loop(0, ny // 2, pair, 0)

    y_parts[0] = parts[0]
    y_tops[0] = part_tops[0]
    remote(parts.at[1:ny], y_parts.at[1:ny], *family(5), sibling).wait_recv()
    remote(part_tops.at[1:ny], y_tops.at[1:ny], *family(6), sibling).wait_recv()
    stats = [y_tops[d] for d in range(ny)]
    row_top = functools.reduce(jnp.maximum, stats)
    stats = [jnp.exp2(stat - row_top) for stat in stats]
    total = functools.reduce(jnp.add, stats)
    inverse = 1.0 / total
    result = jnp.zeros((line, head_dim), jnp.float32)
    for d in range(ny):
        spread = jnp.where(eye, stats[d] * inverse, 0.0).astype(jnp.bfloat16)
        result = result + dot(spread, y_parts[d].reshape(line, head_dim))
    merged[...] = result.astype(jnp.bfloat16).reshape(nx, rows, head_dim)
    merged_top[...] = row_top + jnp.log2(total)
    for d in range(1, nx):
        p_x(d).start()
        pt_x(d).start()
    x_parts[0] = merged[0]
    x_tops[0] = merged_top[...]
    remote(merged.at[1:nx], x_parts.at[1:nx], *family(7), sibling).wait_recv()
    remote(x_tops.at[1:nx], x_tops.at[1:nx], *family(8), sibling).wait_recv()

    lane_row = lax.broadcasted_iota(jnp.int32, (1, LANES), 1)
    flat = x_tops[0]
    for d in range(1, nx):
        flat = jnp.where(lax.div(lane_row, rows) == d, x_tops[d], flat)

    def over_groups(result, op):
        turn = LANES // 2
        while turn >= rows:
            result = op(result, pltpu.roll(result, turn, 1))
            turn //= 2
        return result

    own_top = suffix_top[...]
    row_top = jnp.maximum(over_groups(flat, jnp.maximum), own_top)
    flat = jnp.exp2(flat - row_top)
    own_weight = jnp.exp2(own_top - row_top)
    inverse = 1.0 / (over_groups(flat, jnp.add) + own_weight)
    own_column = jnp.sum(
        jnp.where(lane == sub, own_weight * inverse, 0.0), axis=1, keepdims=True
    )
    spread = jnp.where(lax.rem(lane, rows) == sub, flat * inverse, 0.0).astype(jnp.bfloat16)
    result = own_column * suffix_part[...] + dot(spread, x_parts[...].reshape(line, head_dim))
    abuf[0, 0] = result.astype(jnp.bfloat16)

    for d in order:
        a_y(d).start()
    w_core().wait_recv()
    local[7].wait()
    remote(abuf.at[0, 1:ny], abuf.at[0, 1:ny], *family(9), sibling).wait_recv()
    for d in range(1, nx):
        a_x(d).start()

    share = ny * tokens * nx // nz

    def project(dx):
        for d in range(ny):
            place = pl.multiple_of(lax.rem(y0 - d + ny, ny) * rows, rows)
            attention32[dx, pl.ds(place, rows), :] = abuf[dx, d].astype(jnp.float32)
        features = jnp.concatenate(
            [
                attention32[dx, pl.ds(h, ny * tokens, stride=heads), :].astype(jnp.bfloat16)
                for h in range(heads)
            ],
            axis=1,
        )
        for cross in range(CORES):
            terms = dot(features, wbuf[cross]).astype(jnp.bfloat16)
            for j in range(nz // nx):
                z_send[dx, j, cross] = terms[j * share : (j + 1) * share]
        for j in range(nz // nx):
            z, copy = z_copy(dx, j, 0)
            z_copy(dx, j, 1)[1].start()

            @pl.when(z != z0)
            def _():
                copy.start()

            @pl.when(z == z0)
            def _():
                z_parts[z0 * CORES + c0] = z_send[dx, j, 0]

    project(0)
    for dx in sorted(range(1, nx), key=lambda d: min(d, nx - d)):
        a_x(dx).wait_recv()
        project(dx)

    sources = nz * CORES
    remote(z_parts.at[1:sources], z_parts.at[1:sources], *family(11), sibling).wait_recv()
    total = []
    for c in range(CORES):
        terms = z_parts[c].astype(jnp.float32)
        for z in range(1, nz):
            terms = terms + z_parts[z * CORES + c].astype(jnp.float32)
        total.append(terms.astype(jnp.bfloat16))
    row_out = lax.broadcasted_iota(jnp.int32, (CORES * share, CORES * share), 0)
    row_in = lax.broadcasted_iota(jnp.int32, (CORES * share, CORES * share), 1)
    core = lax.rem(lax.div(row_out, tokens), CORES)
    source = (
        core * share + lax.div(row_out, CORES * tokens) * tokens + lax.rem(row_out, tokens)
    )
    reorder = jnp.where(row_in == source, 1.0, 0.0).astype(jnp.bfloat16)
    out_ref[...] = dot(reorder, jnp.concatenate(total, axis=0)).astype(jnp.bfloat16)

    remote(qbuf.at[0, 1:nx], qbuf.at[0, 1:nx], *family(0), sibling).wait_send()
    remote(qbuf.at[1:ny], qbuf.at[1:ny], send_sem.at[1], qy_sem.at[1], sibling).wait_send()
    for copy in (k_core, v_core, w_core):
        copy().wait_send()
    remote(parts.at[1:ny], y_parts.at[1:ny], *family(5), sibling).wait_send()
    remote(part_tops.at[1:ny], y_tops.at[1:ny], *family(6), sibling).wait_send()
    remote(merged.at[1:nx], x_parts.at[1:nx], *family(7), sibling).wait_send()
    remote(x_tops.at[1:nx], x_tops.at[1:nx], *family(8), sibling).wait_send()
    remote(abuf.at[0, 1:ny], abuf.at[0, 1:ny], *family(9), sibling).wait_send()
    remote(abuf.at[1:nx], abuf.at[1:nx], send_sem.at[10], recv_sem.at[10], sibling).wait_send()
    remote(z_parts.at[1:sources], z_parts.at[1:sources], *family(11), sibling).wait_send()


def per_device(
    sizes,
    queries,
    prefix_keys,
    prefix_values,
    suffix_keys,
    suffix_values,
    new_keys,
    new_values,
    suffix_lengths,
    out_weight,
):
    nx, ny, nz = sizes
    samp_dev, steps, heads, head_dim = queries.shape
    rows = samp_dev * steps * heads
    tokens = samp_dev * steps
    keys = prefix_keys.shape[0]
    slots = suffix_keys.shape[1]
    columns = out_weight.shape[1]
    share = ny * tokens * nx // nz
    bf16, f32 = jnp.bfloat16, jnp.float32
    anywhere = pl.BlockSpec(memory_space=pl.ANY)
    out = pl.pallas_call(
        functools.partial(attend_kernel, sizes),
        out_shape=jax.ShapeDtypeStruct((CORES * share, columns), bf16),
        in_specs=[anywhere] * 7 + [pl.BlockSpec(memory_space=pltpu.SMEM), anywhere],
        out_specs=pl.BlockSpec(memory_space=pltpu.VMEM),
        scratch_shapes=[
            pltpu.VMEM((CORES, keys, head_dim), bf16),
            pltpu.VMEM((CORES, keys, head_dim + LANES), bf16),
            pltpu.VMEM((samp_dev, slots, head_dim), bf16),
            pltpu.VMEM((samp_dev, slots, head_dim), bf16),
            pltpu.VMEM((samp_dev, steps, head_dim), bf16),
            pltpu.VMEM((samp_dev, steps, head_dim), bf16),
            pltpu.VMEM((CORES, heads * head_dim, columns), bf16),
            pltpu.VMEM((ny, nx, rows, head_dim), bf16),
            pltpu.VMEM((ny, nx, rows, head_dim), bf16),
            pltpu.VMEM((ny, 1, LANES), f32),
            pltpu.VMEM((ny, nx, rows, head_dim), bf16),
            pltpu.VMEM((ny, 1, LANES), f32),
            pltpu.VMEM((nx, rows, head_dim), bf16),
            pltpu.VMEM((1, LANES), f32),
            pltpu.VMEM((nx, rows, head_dim), bf16),
            pltpu.VMEM((nx, 1, LANES), f32),
            pltpu.VMEM((rows, head_dim), f32),
            pltpu.VMEM((1, LANES), f32),
            pltpu.VMEM((nx, ny, rows, head_dim), bf16),
            pltpu.VMEM((nx, ny * rows, head_dim), f32),
            pltpu.VMEM((nx, nz // nx, CORES, share, columns), bf16),
            pltpu.VMEM((nz * CORES, share, columns), bf16),
            pltpu.SemaphoreType.DMA((8,)),
            pltpu.SemaphoreType.DMA((12,)),
            pltpu.SemaphoreType.DMA((11 + nx,)),
            pltpu.SemaphoreType.DMA((ny,)),
        ],
        compiler_params=pltpu.CompilerParams(
            collective_id=0, has_side_effects=True, vmem_limit_bytes=60 * 1024 * 1024
        ),
    )(
        queries.reshape(rows, head_dim),
        prefix_keys.reshape(keys, head_dim),
        prefix_values.reshape(keys, head_dim),
        suffix_keys.reshape(samp_dev, slots, head_dim),
        suffix_values.reshape(samp_dev, slots, head_dim),
        new_keys.reshape(samp_dev, steps, head_dim),
        new_values.reshape(samp_dev, steps, head_dim),
        suffix_lengths,
        out_weight,
    )
    return out.reshape(CORES * share // steps, steps, columns)


def solution(mesh, sizes=(4, 8, 8)):
    placed = (
        P("ctx", None, "tp", None),
        P("ctx", "tp", None),
        P("ctx", "tp", None),
        P("ctx", None, "tp", None),
        P("ctx", None, "tp", None),
        P("ctx", None, "tp", None),
        P("ctx", None, "tp", None),
        P("ctx"),
        P("tp", "ctx"),
    )
    return jax.shard_map(
        functools.partial(per_device, sizes),
        mesh=mesh,
        in_specs=placed,
        out_specs=P("tp", None, "ctx"),
        check_vma=False,
    )
```

```python
import functools
import math

import jax
import jax.numpy as jnp
from jax import lax
from jax.experimental import pallas as pl
from jax.experimental.pallas import tpu as pltpu
from jax.sharding import PartitionSpec as P

MESH = pl.DeviceIdType.MESH
LANES = 128
CORES = 2
masked_score = -1e30


def dot_rows(left, right):
    return lax.dot_general(
        left, right, (((1,), (1,)), ((), ())), preferred_element_type=jnp.float32
    )


def dot(left, right):
    return jnp.dot(left, right, preferred_element_type=jnp.float32)


def attend_kernel(
    sizes,
    q_ref,
    k_ref,
    v_ref,
    sk_ref,
    sv_ref,
    nk_ref,
    nv_ref,
    len_ref,
    w_ref,
    out_ref,
    kbuf,
    vbuf,
    skbuf,
    svbuf,
    nkbuf,
    nvbuf,
    wbuf,
    qbuf,
    parts,
    part_tops,
    got,
    got_tops,
    suffix_part,
    suffix_top,
    abuf,
    attention32,
    z_send,
    z_parts,
    local_sem,
    send_sem,
    recv_sem,
    q_sem,
):
    nx, ny, nz = sizes
    rows, head_dim = q_ref.shape
    samp_dev, slots = sk_ref.shape[0], sk_ref.shape[1]
    keys = k_ref.shape[0]
    samp_rows = rows // samp_dev
    steps = nk_ref.shape[1]
    heads = samp_rows // steps
    tokens = rows // heads
    line = nx * rows
    log2_scale = (head_dim ** (-0.5)) * math.log2(math.e)

    me = lax.axis_index("ctx")
    z0 = lax.axis_index("tp")
    c0 = lax.rem(me, CORES)
    y0 = lax.rem(lax.div(me, CORES), ny)
    x0 = lax.div(me, CORES * ny)

    def at(x, y, c):
        return {"ctx": (x * ny + y) * CORES + c}

    def peer(dx, dy):
        return at(lax.rem(x0 + dx + nx, nx), lax.rem(y0 + dy + ny, ny), c0)

    def x_peer(d):
        return peer(d, 0)

    def y_peer(d):
        return peer(0, d)

    sibling = at(x0, y0, 1 - c0)
    z_same = lax.axis_index("ctx")
    z_cross = (x0 * ny + y0) * CORES + 1 - c0

    def remote(src, dst, send, recv, device):
        return pltpu.make_async_remote_copy(
            src_ref=src,
            dst_ref=dst,
            send_sem=send,
            recv_sem=recv,
            device_id=device,
            device_id_type=MESH,
        )

    def family(number):
        return send_sem.at[number], recv_sem.at[number]

    def q_copy(dx, dy):
        return remote(
            qbuf.at[0, 0], qbuf.at[dy, dx], send_sem.at[0], q_sem.at[dy], peer(dx, dy)
        )

    def k_core():
        return remote(k_ref, kbuf.at[1], *family(2), sibling)

    def v_core():
        return remote(v_ref, vbuf.at[1, :, 0:head_dim], *family(3), sibling)

    def w_core():
        return remote(w_ref, wbuf.at[1], *family(4), sibling)

    def p_copy(dx, dy):
        return remote(parts.at[dy, dx], got.at[dy, dx], *family(5), peer(-dx, -dy))

    def pt_copy(dx, dy):
        return remote(part_tops.at[dy], got_tops.at[dy, dx], *family(6), peer(-dx, -dy))

    def own_line_copy(dx):
        return (
            remote(parts.at[0, dx], got.at[0, dx], *family(7), peer(-dx, 0)),
            remote(part_tops.at[0], got_tops.at[0, dx], *family(8), peer(-dx, 0)),
        )

    def a_y(d):
        return remote(abuf.at[0, 0], abuf.at[0, d], *family(9), y_peer(d))

    def a_x(d):
        return remote(abuf.at[0], abuf.at[d], send_sem.at[10], recv_sem.at[11 + d], x_peer(d))

    def z_copy(dx, j, cross):
        z = lax.rem(x0 - dx + nx, nx) * (nz // nx) + j
        return z, remote(
            z_send.at[dx, j, cross],
            z_parts.at[z0 * CORES + c0],
            *family(11),
            {"ctx": z_cross if cross else z_same, "tp": z},
        )

    barrier = pltpu.get_barrier_semaphore()
    order = sorted(range(1, ny), key=lambda d: -min(d, ny - d))
    others = [(dx, dy) for dy in [*range(1, ny), 0] for dx in range(nx) if dx or dy]
    others.sort(key=lambda d: -min(d[0], nx - d[0]) - min(d[1], ny - d[1]))
    partners = [peer(dx, dy) for dx, dy in others] + [sibling]
    for d in sorted(range(1, nz), key=lambda d: -min(d, nz - d)):
        z = lax.rem(z0 + d, nz)
        partners += [{"ctx": z_same, "tp": z}, {"ctx": z_cross, "tp": z}]
    for partner in partners:
        pl.semaphore_signal(barrier, inc=1, device_id=partner, device_id_type=MESH)

    local = [
        pltpu.make_async_copy(q_ref, qbuf.at[0, 0], local_sem.at[0]),
        pltpu.make_async_copy(sk_ref, skbuf, local_sem.at[1]),
        pltpu.make_async_copy(nk_ref, nkbuf, local_sem.at[2]),
        pltpu.make_async_copy(nv_ref, nvbuf, local_sem.at[3]),
        pltpu.make_async_copy(sv_ref, svbuf, local_sem.at[4]),
        pltpu.make_async_copy(k_ref, kbuf.at[0], local_sem.at[5]),
        pltpu.make_async_copy(v_ref, vbuf.at[0, :, 0:head_dim], local_sem.at[6]),
        pltpu.make_async_copy(w_ref, wbuf.at[0], local_sem.at[7]),
    ]
    for copy in local:
        copy.start()
    for c in range(CORES):
        vbuf[c, :, head_dim:] = jnp.ones((keys, LANES), jnp.bfloat16)

    pl.semaphore_wait(barrier, len(partners))
    local[0].wait()
    for dy in [*range(1, ny), 0]:
        for dx in range(nx):
            if dx or dy:
                q_copy(dx, dy).start()
    k_core().start()
    v_core().start()

    for copy in local[1:5]:
        copy.wait()
    own_queries = qbuf[0, 0]
    row_in_sample = lax.broadcasted_iota(jnp.int32, (samp_rows, 1), 0)
    slot_index = lax.broadcasted_iota(jnp.int32, (samp_rows, slots), 1)
    tops = []
    for s in range(samp_dev):
        queries = own_queries[s * samp_rows : (s + 1) * samp_rows]
        scores = dot_rows(queries, skbuf[s])
        scores = jnp.where(slot_index < len_ref[s], scores, masked_score)
        new_keys = nkbuf[s].astype(jnp.float32)
        new_values = nvbuf[s].astype(jnp.float32)
        row_top = jnp.max(scores, axis=1, keepdims=True)
        recent = []
        for u in range(steps):
            score = jnp.sum(
                queries.astype(jnp.float32) * new_keys[u : u + 1], axis=1, keepdims=True
            )
            score = jnp.where(row_in_sample >= u * heads, score, masked_score)
            row_top = jnp.maximum(row_top, score)
            recent.append(score)
        weights = jnp.exp2((scores - row_top) * log2_scale)
        row_total = jnp.sum(weights, axis=1, keepdims=True)
        weighted = dot(weights.astype(jnp.bfloat16), svbuf[s])
        for u in range(steps):
            weight = jnp.exp2((recent[u] - row_top) * log2_scale)
            row_total = row_total + weight
            weighted = weighted + weight.astype(jnp.bfloat16).astype(jnp.float32) * (
                new_values[u : u + 1]
            )
        suffix_part[s * samp_rows : (s + 1) * samp_rows, :] = weighted / row_total
        tops.append(row_top * log2_scale + jnp.log2(row_total))
    lane = lax.broadcasted_iota(jnp.int32, (rows, LANES), 1)
    sub = lax.broadcasted_iota(jnp.int32, (rows, LANES), 0)
    suffix_top[...] = jnp.sum(
        jnp.where(lax.rem(lane, rows) == sub, jnp.concatenate(tops, axis=0), 0.0),
        axis=0,
        keepdims=True,
    )

    local[5].wait()
    local[6].wait()
    k_core().wait_recv()
    v_core().wait_recv()
    w_core().start()

    eye = lax.broadcasted_iota(jnp.int32, (LANES, LANES), 0) == lax.broadcasted_iota(
        jnp.int32, (LANES, LANES), 1
    )
    width = min(keys, 256)

    def attend(queries):
        row_top = weighted = None
        for c in range(CORES):
            for start in range(0, keys, width):
                scores = dot_rows(queries, kbuf[c, start : start + width])
                block_top = jnp.max(scores, axis=1, keepdims=True)
                top = block_top if row_top is None else jnp.maximum(row_top, block_top)
                weights = jnp.exp2((scores - top) * log2_scale).astype(jnp.bfloat16)
                term = dot(weights, vbuf[c, start : start + width])
                if row_top is not None:
                    term = weighted * jnp.exp2((row_top - top) * log2_scale) + term
                row_top, weighted = top, term
        total = weighted[:, head_dim:]
        part = (weighted[:, :head_dim] / total).astype(jnp.bfloat16)
        return part, row_top * log2_scale + jnp.log2(total)

    def line_arrived(dy):
        return remote(qbuf.at[dy], qbuf.at[dy], send_sem.at[0], q_sem.at[dy], sibling)

    def pair(k, carry):
        first, second = 2 * k + 1, lax.rem(2 * k + 2, ny)
        line_arrived(first).wait_recv()

        @pl.when(second != 0)
        def _():
            line_arrived(second).wait_recv()

        @pl.when(second == 0)
        def _():
            mine = qbuf.at[0, 1:nx]
            remote(mine, mine, send_sem.at[0], q_sem.at[0], sibling).wait_recv()

        queries = jnp.concatenate(
            [qbuf[first].reshape(line, head_dim), qbuf[second].reshape(line, head_dim)], axis=0
        )
        part, top = attend(queries)
        for i, slot in enumerate((first, second)):
            parts[slot] = part[i * line : (i + 1) * line].reshape(nx, rows, head_dim)
            part_tops[slot] = jnp.sum(
                jnp.where(eye, top[i * line : (i + 1) * line], 0.0), axis=0, keepdims=True
            )
        for dx in range(nx):
            p_copy(dx, first).start()
            pt_copy(dx, first).start()

        @pl.when(second != 0)
        def _():
            for dx in range(nx):
                p_copy(dx, second).start()
                pt_copy(dx, second).start()

        return carry

    lax.fori_loop(0, ny // 2, pair, 0)

    for dx in range(1, nx):
        for copy in own_line_copy(dx):
            copy.start()
    got[0, 0] = parts[0, 0]
    got_tops[0, 0] = part_tops[0]
    arrivals = (
        (got.at[1:ny], *family(5)),
        (got_tops.at[1:ny], *family(6)),
        (got.at[0, 1:nx], *family(7)),
        (got_tops.at[0, 1:nx], *family(8)),
    )
    for ref, send, recv in arrivals:
        remote(ref, ref, send, recv, sibling).wait_recv()

    lane_row = lax.broadcasted_iota(jnp.int32, (1, LANES), 1)
    stats = []
    for dy in range(ny):
        flat = got_tops[dy, 0]
        for dx in range(1, nx):
            flat = jnp.where(lax.div(lane_row, rows) == dx, got_tops[dy, dx], flat)
        stats.append(flat)

    def over_groups(result, op):
        turn = LANES // 2
        while turn >= rows:
            result = op(result, pltpu.roll(result, turn, 1))
            turn //= 2
        return result

    own_top = suffix_top[...]
    row_top = jnp.maximum(
        over_groups(functools.reduce(jnp.maximum, stats), jnp.maximum), own_top
    )
    stats = [jnp.exp2(flat - row_top) for flat in stats]
    own_weight = jnp.exp2(own_top - row_top)
    inverse = 1.0 / (over_groups(functools.reduce(jnp.add, stats), jnp.add) + own_weight)
    own_column = jnp.sum(
        jnp.where(lane == sub, own_weight * inverse, 0.0), axis=1, keepdims=True
    )
    result = own_column * suffix_part[...]
    for dy in range(ny):
        spread = jnp.where(lax.rem(lane, rows) == sub, stats[dy] * inverse, 0.0)
        result = result + dot(spread.astype(jnp.bfloat16), got[dy].reshape(line, head_dim))
    abuf[0, 0] = result.astype(jnp.bfloat16)

    for d in order:
        a_y(d).start()
    w_core().wait_recv()
    local[7].wait()
    remote(abuf.at[0, 1:ny], abuf.at[0, 1:ny], *family(9), sibling).wait_recv()
    for d in range(1, nx):
        a_x(d).start()

    share = ny * tokens * nx // nz

    def project(dx):
        for d in range(ny):
            place = pl.multiple_of(lax.rem(y0 - d + ny, ny) * rows, rows)
            attention32[dx, pl.ds(place, rows), :] = abuf[dx, d].astype(jnp.float32)
        features = jnp.concatenate(
            [
                attention32[dx, pl.ds(h, ny * tokens, stride=heads), :].astype(jnp.bfloat16)
                for h in range(heads)
            ],
            axis=1,
        )
        for cross in range(CORES):
            terms = dot(features, wbuf[cross]).astype(jnp.bfloat16)
            for j in range(nz // nx):
                z_send[dx, j, cross] = terms[j * share : (j + 1) * share]
        for j in range(nz // nx):
            z, copy = z_copy(dx, j, 0)
            z_copy(dx, j, 1)[1].start()

            @pl.when(z != z0)
            def _():
                copy.start()

            @pl.when(z == z0)
            def _():
                z_parts[z0 * CORES + c0] = z_send[dx, j, 0]

    project(0)
    for dx in sorted(range(1, nx), key=lambda d: min(d, nx - d)):
        a_x(dx).wait_recv()
        project(dx)

    sources = nz * CORES
    remote(z_parts.at[1:sources], z_parts.at[1:sources], *family(11), sibling).wait_recv()
    total = []
    for c in range(CORES):
        terms = z_parts[c].astype(jnp.float32)
        for z in range(1, nz):
            terms = terms + z_parts[z * CORES + c].astype(jnp.float32)
        total.append(terms.astype(jnp.bfloat16))
    row_out = lax.broadcasted_iota(jnp.int32, (CORES * share, CORES * share), 0)
    row_in = lax.broadcasted_iota(jnp.int32, (CORES * share, CORES * share), 1)
    core = lax.rem(lax.div(row_out, tokens), CORES)
    source = (
        core * share + lax.div(row_out, CORES * tokens) * tokens + lax.rem(row_out, tokens)
    )
    reorder = jnp.where(row_in == source, 1.0, 0.0).astype(jnp.bfloat16)
    out_ref[...] = dot(reorder, jnp.concatenate(total, axis=0)).astype(jnp.bfloat16)

    sent = qbuf.at[1:ny]
    remote(sent, sent, send_sem.at[0], q_sem.at[1], sibling).wait_send()
    sent = qbuf.at[0, 1:nx]
    remote(sent, sent, send_sem.at[0], q_sem.at[0], sibling).wait_send()
    for copy in (k_core, v_core, w_core):
        copy().wait_send()
    for ref, send, recv in arrivals:
        remote(ref, ref, send, recv, sibling).wait_send()
    remote(abuf.at[0, 1:ny], abuf.at[0, 1:ny], *family(9), sibling).wait_send()
    remote(abuf.at[1:nx], abuf.at[1:nx], send_sem.at[10], recv_sem.at[10], sibling).wait_send()
    remote(z_parts.at[1:sources], z_parts.at[1:sources], *family(11), sibling).wait_send()


def per_device(
    sizes,
    queries,
    prefix_keys,
    prefix_values,
    suffix_keys,
    suffix_values,
    new_keys,
    new_values,
    suffix_lengths,
    out_weight,
):
    nx, ny, nz = sizes
    samp_dev, steps, heads, head_dim = queries.shape
    rows = samp_dev * steps * heads
    tokens = samp_dev * steps
    keys = prefix_keys.shape[0]
    slots = suffix_keys.shape[1]
    columns = out_weight.shape[1]
    share = ny * tokens * nx // nz
    bf16, f32 = jnp.bfloat16, jnp.float32
    anywhere = pl.BlockSpec(memory_space=pl.ANY)
    out = pl.pallas_call(
        functools.partial(attend_kernel, sizes),
        out_shape=jax.ShapeDtypeStruct((CORES * share, columns), bf16),
        in_specs=[anywhere] * 7 + [pl.BlockSpec(memory_space=pltpu.SMEM), anywhere],
        out_specs=pl.BlockSpec(memory_space=pltpu.VMEM),
        scratch_shapes=[
            pltpu.VMEM((CORES, keys, head_dim), bf16),
            pltpu.VMEM((CORES, keys, head_dim + LANES), bf16),
            pltpu.VMEM((samp_dev, slots, head_dim), bf16),
            pltpu.VMEM((samp_dev, slots, head_dim), bf16),
            pltpu.VMEM((samp_dev, steps, head_dim), bf16),
            pltpu.VMEM((samp_dev, steps, head_dim), bf16),
            pltpu.VMEM((CORES, heads * head_dim, columns), bf16),
            pltpu.VMEM((ny, nx, rows, head_dim), bf16),
            pltpu.VMEM((ny, nx, rows, head_dim), bf16),
            pltpu.VMEM((ny, 1, LANES), f32),
            pltpu.VMEM((ny, nx, rows, head_dim), bf16),
            pltpu.VMEM((ny, nx, 1, LANES), f32),
            pltpu.VMEM((rows, head_dim), f32),
            pltpu.VMEM((1, LANES), f32),
            pltpu.VMEM((nx, ny, rows, head_dim), bf16),
            pltpu.VMEM((nx, ny * rows, head_dim), f32),
            pltpu.VMEM((nx, nz // nx, CORES, share, columns), bf16),
            pltpu.VMEM((nz * CORES, share, columns), bf16),
            pltpu.SemaphoreType.DMA((8,)),
            pltpu.SemaphoreType.DMA((12,)),
            pltpu.SemaphoreType.DMA((11 + nx,)),
            pltpu.SemaphoreType.DMA((ny,)),
        ],
        compiler_params=pltpu.CompilerParams(
            collective_id=0, has_side_effects=True, vmem_limit_bytes=60 * 1024 * 1024
        ),
    )(
        queries.reshape(rows, head_dim),
        prefix_keys.reshape(keys, head_dim),
        prefix_values.reshape(keys, head_dim),
        suffix_keys.reshape(samp_dev, slots, head_dim),
        suffix_values.reshape(samp_dev, slots, head_dim),
        new_keys.reshape(samp_dev, steps, head_dim),
        new_values.reshape(samp_dev, steps, head_dim),
        suffix_lengths,
        out_weight,
    )
    return out.reshape(CORES * share // steps, steps, columns)


def solution(mesh, sizes=(4, 8, 8)):
    placed = (
        P("ctx", None, "tp", None),
        P("ctx", "tp", None),
        P("ctx", "tp", None),
        P("ctx", None, "tp", None),
        P("ctx", None, "tp", None),
        P("ctx", None, "tp", None),
        P("ctx", None, "tp", None),
        P("ctx"),
        P("tp", "ctx"),
    )
    return jax.shard_map(
        functools.partial(per_device, sizes),
        mesh=mesh,
        in_specs=placed,
        out_specs=P("tp", None, "ctx"),
        check_vma=False,
    )
```

```python
import functools
import math

import jax
import jax.numpy as jnp
from jax import lax
from jax.experimental import pallas as pl
from jax.experimental.pallas import tpu as pltpu
from jax.sharding import PartitionSpec as P

MESH = pl.DeviceIdType.MESH
LANES = 128
CORES = 2
masked_score = -1e30


def dot_rows(left, right):
    return lax.dot_general(
        left, right, (((1,), (1,)), ((), ())), preferred_element_type=jnp.float32
    )


def dot(left, right):
    return jnp.dot(left, right, preferred_element_type=jnp.float32)


def attend_kernel(
    sizes,
    q_ref,
    k_ref,
    v_ref,
    sk_ref,
    sv_ref,
    nk_ref,
    nv_ref,
    len_ref,
    w_ref,
    out_ref,
    kbuf,
    vbuf,
    skbuf,
    svbuf,
    nkbuf,
    nvbuf,
    wbuf,
    qbuf,
    parts,
    part_tops,
    got,
    got_tops,
    suffix_part,
    suffix_top,
    abuf,
    attention32,
    z_send,
    z_parts,
    local_sem,
    send_sem,
    recv_sem,
    q_sem,
    a_sem,
):
    nx, ny, nz = sizes
    rows, head_dim = q_ref.shape
    samp_dev, slots = sk_ref.shape[0], sk_ref.shape[1]
    keys = k_ref.shape[0]
    samp_rows = rows // samp_dev
    steps = nk_ref.shape[1]
    heads = samp_rows // steps
    tokens = rows // heads
    line = nx * rows
    log2_scale = (head_dim ** (-0.5)) * math.log2(math.e)

    me = lax.axis_index("ctx")
    z0 = lax.axis_index("tp")
    c0 = lax.rem(me, CORES)
    y0 = lax.rem(lax.div(me, CORES), ny)
    x0 = lax.div(me, CORES * ny)

    def at(x, y, c):
        return {"ctx": (x * ny + y) * CORES + c}

    def peer(dx, dy):
        return at(lax.rem(x0 + dx + nx, nx), lax.rem(y0 + dy + ny, ny), c0)

    def x_peer(d):
        return peer(d, 0)

    def y_peer(d):
        return peer(0, d)

    sibling = at(x0, y0, 1 - c0)
    far_first = sorted(range(nx), key=lambda d: -min(d, nx - d))
    z_same = lax.axis_index("ctx")
    z_cross = (x0 * ny + y0) * CORES + 1 - c0

    def remote(src, dst, send, recv, device):
        return pltpu.make_async_remote_copy(
            src_ref=src,
            dst_ref=dst,
            send_sem=send,
            recv_sem=recv,
            device_id=device,
            device_id_type=MESH,
        )

    def family(number):
        return send_sem.at[number], recv_sem.at[number]

    def q_copy(dx, dy):
        return remote(
            qbuf.at[0, 0], qbuf.at[dy, dx], send_sem.at[0], q_sem.at[dy], peer(dx, dy)
        )

    def k_core():
        return remote(k_ref, kbuf.at[1], *family(2), sibling)

    def v_core():
        return remote(v_ref, vbuf.at[1, :, 0:head_dim], *family(3), sibling)

    def w_core():
        return remote(w_ref, wbuf.at[1], *family(4), sibling)

    def p_copy(dx, dy):
        return remote(parts.at[dy, dx], got.at[dy, dx], *family(5), peer(-dx, -dy))

    def pt_copy(dx, dy):
        return remote(part_tops.at[dy], got_tops.at[dy, dx], *family(6), peer(-dx, -dy))

    def own_line_copy(dx):
        return (
            remote(parts.at[0, dx], got.at[0, dx], *family(7), peer(-dx, 0)),
            remote(part_tops.at[0], got_tops.at[0, dx], *family(8), peer(-dx, 0)),
        )

    def a_y(d):
        return remote(abuf.at[0, 0], abuf.at[0, d], send_sem.at[9], a_sem.at[d], y_peer(d))

    def a_x(d, dy):
        return remote(
            abuf.at[0, dy], abuf.at[d, dy], send_sem.at[10], recv_sem.at[11 + d], x_peer(d)
        )

    def z_copy(dx, j, cross):
        z = lax.rem(x0 - dx + nx, nx) * (nz // nx) + j
        return z, remote(
            z_send.at[dx, j, cross],
            z_parts.at[z0 * CORES + c0],
            *family(11),
            {"ctx": z_cross if cross else z_same, "tp": z},
        )

    barrier = pltpu.get_barrier_semaphore()
    order = sorted(range(1, ny), key=lambda d: -min(d, ny - d))
    others = [(dx, dy) for dy in [*range(1, ny), 0] for dx in range(nx) if dx or dy]
    others.sort(key=lambda d: -min(d[0], nx - d[0]) - min(d[1], ny - d[1]))
    partners = [peer(dx, dy) for dx, dy in others] + [sibling]
    for d in sorted(range(1, nz), key=lambda d: -min(d, nz - d)):
        z = lax.rem(z0 + d, nz)
        partners += [{"ctx": z_same, "tp": z}, {"ctx": z_cross, "tp": z}]
    for partner in partners:
        pl.semaphore_signal(barrier, inc=1, device_id=partner, device_id_type=MESH)

    local = [
        pltpu.make_async_copy(q_ref, qbuf.at[0, 0], local_sem.at[0]),
        pltpu.make_async_copy(sk_ref, skbuf, local_sem.at[1]),
        pltpu.make_async_copy(nk_ref, nkbuf, local_sem.at[2]),
        pltpu.make_async_copy(nv_ref, nvbuf, local_sem.at[3]),
        pltpu.make_async_copy(sv_ref, svbuf, local_sem.at[4]),
        pltpu.make_async_copy(k_ref, kbuf.at[0], local_sem.at[5]),
        pltpu.make_async_copy(v_ref, vbuf.at[0, :, 0:head_dim], local_sem.at[6]),
        pltpu.make_async_copy(w_ref, wbuf.at[0], local_sem.at[7]),
    ]
    for copy in local:
        copy.start()
    for c in range(CORES):
        vbuf[c, :, head_dim:] = jnp.ones((keys, LANES), jnp.bfloat16)

    pl.semaphore_wait(barrier, len(partners))
    local[0].wait()
    lines = []
    for k in range(ny // 2):
        first = 1 + (k + 1) % (ny // 2)
        lines += [first, (ny - first) * (1 - first // (ny // 2))]
    for dy in lines:
        for dx in far_first:
            if dx or dy:
                q_copy(dx, dy).start()
    k_core().start()
    v_core().start()

    for copy in local[1:5]:
        copy.wait()
    own_queries = qbuf[0, 0]
    row_in_sample = lax.broadcasted_iota(jnp.int32, (samp_rows, 1), 0)
    slot_index = lax.broadcasted_iota(jnp.int32, (samp_rows, slots), 1)
    tops = []
    for s in range(samp_dev):
        queries = own_queries[s * samp_rows : (s + 1) * samp_rows]
        scores = dot_rows(queries, skbuf[s])
        scores = jnp.where(slot_index < len_ref[s], scores, masked_score)
        new_keys = nkbuf[s].astype(jnp.float32)
        new_values = nvbuf[s].astype(jnp.float32)
        row_top = jnp.max(scores, axis=1, keepdims=True)
        recent = []
        for u in range(steps):
            score = jnp.sum(
                queries.astype(jnp.float32) * new_keys[u : u + 1], axis=1, keepdims=True
            )
            score = jnp.where(row_in_sample >= u * heads, score, masked_score)
            row_top = jnp.maximum(row_top, score)
            recent.append(score)
        weights = jnp.exp2((scores - row_top) * log2_scale)
        row_total = jnp.sum(weights, axis=1, keepdims=True)
        weighted = dot(weights.astype(jnp.bfloat16), svbuf[s])
        for u in range(steps):
            weight = jnp.exp2((recent[u] - row_top) * log2_scale)
            row_total = row_total + weight
            weighted = weighted + weight.astype(jnp.bfloat16).astype(jnp.float32) * (
                new_values[u : u + 1]
            )
        suffix_part[s * samp_rows : (s + 1) * samp_rows, :] = weighted / row_total
        tops.append(row_top * log2_scale + jnp.log2(row_total))
    lane = lax.broadcasted_iota(jnp.int32, (rows, LANES), 1)
    sub = lax.broadcasted_iota(jnp.int32, (rows, LANES), 0)
    suffix_top[...] = jnp.sum(
        jnp.where(lax.rem(lane, rows) == sub, jnp.concatenate(tops, axis=0), 0.0),
        axis=0,
        keepdims=True,
    )

    local[5].wait()
    local[6].wait()
    k_core().wait_recv()
    v_core().wait_recv()
    w_core().start()

    eye = lax.broadcasted_iota(jnp.int32, (LANES, LANES), 0) == lax.broadcasted_iota(
        jnp.int32, (LANES, LANES), 1
    )
    width = min(keys, 256)

    def attend(queries):
        row_top = weighted = None
        for c in range(CORES):
            for start in range(0, keys, width):
                scores = dot_rows(queries, kbuf[c, start : start + width])
                block_top = jnp.max(scores, axis=1, keepdims=True)
                top = block_top if row_top is None else jnp.maximum(row_top, block_top)
                weights = jnp.exp2((scores - top) * log2_scale).astype(jnp.bfloat16)
                term = dot(weights, vbuf[c, start : start + width])
                if row_top is not None:
                    term = weighted * jnp.exp2((row_top - top) * log2_scale) + term
                row_top, weighted = top, term
        total = weighted[:, head_dim:]
        part = (weighted[:, :head_dim] / total).astype(jnp.bfloat16)
        return part, row_top * log2_scale + jnp.log2(total)

    def line_arrived(dy):
        return remote(qbuf.at[dy], qbuf.at[dy], send_sem.at[0], q_sem.at[dy], sibling)

    half = ny // 2

    def pair(k, carry):
        first = 1 + lax.rem(k + 1, half)
        second = (ny - first) * (1 - lax.div(first, half))
        line_arrived(first).wait_recv()

        @pl.when(second != 0)
        def _():
            line_arrived(second).wait_recv()

        @pl.when(second == 0)
        def _():
            mine = qbuf.at[0, 1:nx]
            remote(mine, mine, send_sem.at[0], q_sem.at[0], sibling).wait_recv()

        queries = jnp.concatenate(
            [qbuf[first].reshape(line, head_dim), qbuf[second].reshape(line, head_dim)], axis=0
        )
        part, top = attend(queries)
        for i, slot in enumerate((first, second)):
            parts[slot] = part[i * line : (i + 1) * line].reshape(nx, rows, head_dim)
            part_tops[slot] = jnp.sum(
                jnp.where(eye, top[i * line : (i + 1) * line], 0.0), axis=0, keepdims=True
            )
        for dx in far_first:
            p_copy(dx, first).start()
            pt_copy(dx, first).start()

        @pl.when(second != 0)
        def _():
            for dx in far_first:
                p_copy(dx, second).start()
                pt_copy(dx, second).start()

        @pl.when(second == 0)
        def _():
            for dx in far_first:
                if dx:
                    for copy in own_line_copy(dx):
                        copy.start()

        return carry

    lax.fori_loop(0, ny // 2, pair, 0)

    got[0, 0] = parts[0, 0]
    got_tops[0, 0] = part_tops[0]
    arrivals = (
        (got.at[1:ny], *family(5)),
        (got_tops.at[1:ny], *family(6)),
        (got.at[0, 1:nx], *family(7)),
        (got_tops.at[0, 1:nx], *family(8)),
    )
    for ref, send, recv in arrivals:
        remote(ref, ref, send, recv, sibling).wait_recv()

    lane_row = lax.broadcasted_iota(jnp.int32, (1, LANES), 1)
    stats = []
    for dy in range(ny):
        flat = got_tops[dy, 0]
        for dx in range(1, nx):
            flat = jnp.where(lax.div(lane_row, rows) == dx, got_tops[dy, dx], flat)
        stats.append(flat)

    def over_groups(result, op):
        turn = LANES // 2
        while turn >= rows:
            result = op(result, pltpu.roll(result, turn, 1))
            turn //= 2
        return result

    own_top = suffix_top[...]
    row_top = jnp.maximum(
        over_groups(functools.reduce(jnp.maximum, stats), jnp.maximum), own_top
    )
    stats = [jnp.exp2(flat - row_top) for flat in stats]
    own_weight = jnp.exp2(own_top - row_top)
    inverse = 1.0 / (over_groups(functools.reduce(jnp.add, stats), jnp.add) + own_weight)
    own_column = jnp.sum(
        jnp.where(lane == sub, own_weight * inverse, 0.0), axis=1, keepdims=True
    )
    result = own_column * suffix_part[...]
    for dy in range(ny):
        spread = jnp.where(lax.rem(lane, rows) == sub, stats[dy] * inverse, 0.0)
        result = result + dot(spread.astype(jnp.bfloat16), got[dy].reshape(line, head_dim))
    abuf[0, 0] = result.astype(jnp.bfloat16)

    for d in order:
        a_y(d).start()
    for d in far_first:
        if d:
            a_x(d, 0).start()
    w_core().wait_recv()
    local[7].wait()
    for dy in reversed(order):
        a_y(dy).wait_recv()
        for d in far_first:
            if d:
                a_x(d, dy).start()

    share = ny * tokens * nx // nz

    def project(dx):
        for d in range(ny):
            place = pl.multiple_of(lax.rem(y0 - d + ny, ny) * rows, rows)
            attention32[dx, pl.ds(place, rows), :] = abuf[dx, d].astype(jnp.float32)
        features = jnp.concatenate(
            [
                attention32[dx, pl.ds(h, ny * tokens, stride=heads), :].astype(jnp.bfloat16)
                for h in range(heads)
            ],
            axis=1,
        )
        for cross in range(CORES):
            terms = dot(features, wbuf[cross]).astype(jnp.bfloat16)
            for j in range(nz // nx):
                z_send[dx, j, cross] = terms[j * share : (j + 1) * share]
        for j in range(nz // nx):
            z, copy = z_copy(dx, j, 0)
            z_copy(dx, j, 1)[1].start()

            @pl.when(z != z0)
            def _():
                copy.start()

            @pl.when(z == z0)
            def _():
                z_parts[z0 * CORES + c0] = z_send[dx, j, 0]

    project(0)
    for dx in sorted(range(1, nx), key=lambda d: min(d, nx - d)):
        came = abuf.at[dx]
        remote(came, came, send_sem.at[10], recv_sem.at[11 + dx], sibling).wait_recv()
        project(dx)

    sources = nz * CORES
    remote(z_parts.at[1:sources], z_parts.at[1:sources], *family(11), sibling).wait_recv()
    total = []
    for c in range(CORES):
        terms = z_parts[c].astype(jnp.float32)
        for z in range(1, nz):
            terms = terms + z_parts[z * CORES + c].astype(jnp.float32)
        total.append(terms.astype(jnp.bfloat16))
    row_out = lax.broadcasted_iota(jnp.int32, (CORES * share, CORES * share), 0)
    row_in = lax.broadcasted_iota(jnp.int32, (CORES * share, CORES * share), 1)
    core = lax.rem(lax.div(row_out, tokens), CORES)
    source = (
        core * share + lax.div(row_out, CORES * tokens) * tokens + lax.rem(row_out, tokens)
    )
    reorder = jnp.where(row_in == source, 1.0, 0.0).astype(jnp.bfloat16)
    out_ref[...] = dot(reorder, jnp.concatenate(total, axis=0)).astype(jnp.bfloat16)

    sent = qbuf.at[1:ny]
    remote(sent, sent, send_sem.at[0], q_sem.at[1], sibling).wait_send()
    sent = qbuf.at[0, 1:nx]
    remote(sent, sent, send_sem.at[0], q_sem.at[0], sibling).wait_send()
    for copy in (k_core, v_core, w_core):
        copy().wait_send()
    for ref, send, recv in arrivals:
        remote(ref, ref, send, recv, sibling).wait_send()
    remote(abuf.at[0, 1:ny], abuf.at[0, 1:ny], send_sem.at[9], a_sem.at[0], sibling).wait_send()
    remote(abuf.at[1:nx], abuf.at[1:nx], send_sem.at[10], recv_sem.at[10], sibling).wait_send()
    remote(z_parts.at[1:sources], z_parts.at[1:sources], *family(11), sibling).wait_send()


def per_device(
    sizes,
    queries,
    prefix_keys,
    prefix_values,
    suffix_keys,
    suffix_values,
    new_keys,
    new_values,
    suffix_lengths,
    out_weight,
):
    nx, ny, nz = sizes
    samp_dev, steps, heads, head_dim = queries.shape
    rows = samp_dev * steps * heads
    tokens = samp_dev * steps
    keys = prefix_keys.shape[0]
    slots = suffix_keys.shape[1]
    columns = out_weight.shape[1]
    share = ny * tokens * nx // nz
    bf16, f32 = jnp.bfloat16, jnp.float32
    anywhere = pl.BlockSpec(memory_space=pl.ANY)
    out = pl.pallas_call(
        functools.partial(attend_kernel, sizes),
        out_shape=jax.ShapeDtypeStruct((CORES * share, columns), bf16),
        in_specs=[anywhere] * 7 + [pl.BlockSpec(memory_space=pltpu.SMEM), anywhere],
        out_specs=pl.BlockSpec(memory_space=pltpu.VMEM),
        scratch_shapes=[
            pltpu.VMEM((CORES, keys, head_dim), bf16),
            pltpu.VMEM((CORES, keys, head_dim + LANES), bf16),
            pltpu.VMEM((samp_dev, slots, head_dim), bf16),
            pltpu.VMEM((samp_dev, slots, head_dim), bf16),
            pltpu.VMEM((samp_dev, steps, head_dim), bf16),
            pltpu.VMEM((samp_dev, steps, head_dim), bf16),
            pltpu.VMEM((CORES, heads * head_dim, columns), bf16),
            pltpu.VMEM((ny, nx, rows, head_dim), bf16),
            pltpu.VMEM((ny, nx, rows, head_dim), bf16),
            pltpu.VMEM((ny, 1, LANES), f32),
            pltpu.VMEM((ny, nx, rows, head_dim), bf16),
            pltpu.VMEM((ny, nx, 1, LANES), f32),
            pltpu.VMEM((rows, head_dim), f32),
            pltpu.VMEM((1, LANES), f32),
            pltpu.VMEM((nx, ny, rows, head_dim), bf16),
            pltpu.VMEM((nx, ny * rows, head_dim), f32),
            pltpu.VMEM((nx, nz // nx, CORES, share, columns), bf16),
            pltpu.VMEM((nz * CORES, share, columns), bf16),
            pltpu.SemaphoreType.DMA((8,)),
            pltpu.SemaphoreType.DMA((12,)),
            pltpu.SemaphoreType.DMA((11 + nx,)),
            pltpu.SemaphoreType.DMA((ny,)),
            pltpu.SemaphoreType.DMA((ny,)),
        ],
        compiler_params=pltpu.CompilerParams(
            collective_id=0, has_side_effects=True, vmem_limit_bytes=60 * 1024 * 1024
        ),
    )(
        queries.reshape(rows, head_dim),
        prefix_keys.reshape(keys, head_dim),
        prefix_values.reshape(keys, head_dim),
        suffix_keys.reshape(samp_dev, slots, head_dim),
        suffix_values.reshape(samp_dev, slots, head_dim),
        new_keys.reshape(samp_dev, steps, head_dim),
        new_values.reshape(samp_dev, steps, head_dim),
        suffix_lengths,
        out_weight,
    )
    return out.reshape(CORES * share // steps, steps, columns)


def solution(mesh, sizes=(4, 8, 8)):
    placed = (
        P("ctx", None, "tp", None),
        P("ctx", "tp", None),
        P("ctx", "tp", None),
        P("ctx", None, "tp", None),
        P("ctx", None, "tp", None),
        P("ctx", None, "tp", None),
        P("ctx", None, "tp", None),
        P("ctx"),
        P("tp", "ctx"),
    )
    return jax.shard_map(
        functools.partial(per_device, sizes),
        mesh=mesh,
        in_specs=placed,
        out_specs=P("tp", None, "ctx"),
        check_vma=False,
    )
```

```python
import functools
import math

import jax
import jax.numpy as jnp
from jax import lax
from jax.experimental import pallas as pl
from jax.experimental.pallas import tpu as pltpu
from jax.sharding import PartitionSpec as P

MESH = pl.DeviceIdType.MESH
LANES = 128
CORES = 2
masked_score = -1e30


def dot_rows(left, right):
    return lax.dot_general(
        left, right, (((1,), (1,)), ((), ())), preferred_element_type=jnp.float32
    )


def dot(left, right):
    return jnp.dot(left, right, preferred_element_type=jnp.float32)


def attend_kernel(
    sizes,
    q_ref,
    k_ref,
    v_ref,
    sk_ref,
    sv_ref,
    nk_ref,
    nv_ref,
    len_ref,
    w_ref,
    out_ref,
    kbuf,
    vbuf,
    skbuf,
    svbuf,
    nkbuf,
    nvbuf,
    wbuf,
    qbuf,
    parts,
    part_tops,
    got,
    got_tops,
    suffix_part,
    suffix_top,
    abuf,
    attention32,
    z_send,
    z_parts,
    local_sem,
    send_sem,
    recv_sem,
    q_sem,
    a_sem,
):
    nx, ny, nz = sizes
    rows, head_dim = q_ref.shape
    samp_dev, slots = sk_ref.shape[0], sk_ref.shape[1]
    keys = k_ref.shape[0]
    samp_rows = rows // samp_dev
    steps = nk_ref.shape[1]
    heads = samp_rows // steps
    tokens = rows // heads
    line = nx * rows
    log2_scale = (head_dim ** (-0.5)) * math.log2(math.e)

    me = lax.axis_index("ctx")
    z0 = lax.axis_index("tp")
    c0 = lax.rem(me, CORES)
    y0 = lax.rem(lax.div(me, CORES), ny)
    x0 = lax.div(me, CORES * ny)

    def at(x, y, c):
        return {"ctx": (x * ny + y) * CORES + c}

    def peer(dx, dy):
        return at(lax.rem(x0 + dx + nx, nx), lax.rem(y0 + dy + ny, ny), c0)

    def x_peer(d):
        return peer(d, 0)

    def y_peer(d):
        return peer(0, d)

    sibling = at(x0, y0, 1 - c0)
    far_first = sorted(range(nx), key=lambda d: -min(d, nx - d))
    z_same = lax.axis_index("ctx")
    z_cross = (x0 * ny + y0) * CORES + 1 - c0

    def remote(src, dst, send, recv, device):
        return pltpu.make_async_remote_copy(
            src_ref=src,
            dst_ref=dst,
            send_sem=send,
            recv_sem=recv,
            device_id=device,
            device_id_type=MESH,
        )

    def family(number):
        return send_sem.at[number], recv_sem.at[number]

    def q_copy(dx, dy):
        return remote(
            qbuf.at[0, 0], qbuf.at[dy, dx], send_sem.at[0], q_sem.at[dy], peer(dx, dy)
        )

    def k_core():
        return remote(k_ref, kbuf.at[1], *family(2), sibling)

    def v_core():
        return remote(v_ref, vbuf.at[1, :, 0:head_dim], *family(3), sibling)

    def w_core():
        return remote(w_ref, wbuf.at[1], *family(4), sibling)

    def p_copy(dx, dy):
        return remote(parts.at[dy, dx], got.at[dy, dx], *family(5), peer(-dx, -dy))

    def pt_copy(dx, dy):
        return remote(part_tops.at[dy], got_tops.at[dy, dx], *family(6), peer(-dx, -dy))

    def own_line_copy(dx):
        return (
            remote(parts.at[0, dx], got.at[0, dx], *family(7), peer(-dx, 0)),
            remote(part_tops.at[0], got_tops.at[0, dx], *family(8), peer(-dx, 0)),
        )

    def a_y(d):
        return remote(abuf.at[0, 0], abuf.at[0, d], send_sem.at[9], a_sem.at[d], y_peer(d))

    def a_x(d, dy):
        return remote(
            abuf.at[0, dy], abuf.at[d, dy], send_sem.at[10], recv_sem.at[11 + d], x_peer(d)
        )

    def z_copy(dx, j, cross):
        z = lax.rem(x0 - dx + nx, nx) * (nz // nx) + j
        return z, remote(
            z_send.at[dx, j, cross],
            z_parts.at[z0 * CORES + c0],
            *family(11),
            {"ctx": z_cross if cross else z_same, "tp": z},
        )

    barrier = pltpu.get_barrier_semaphore()
    order = sorted(range(1, ny), key=lambda d: -min(d, ny - d))
    others = [(dx, dy) for dy in [*range(1, ny), 0] for dx in range(nx) if dx or dy]
    others.sort(key=lambda d: -min(d[0], nx - d[0]) - min(d[1], ny - d[1]))
    partners = [peer(dx, dy) for dx, dy in others] + [sibling]
    for d in sorted(range(1, nz), key=lambda d: -min(d, nz - d)):
        z = lax.rem(z0 + d, nz)
        partners += [{"ctx": z_same, "tp": z}, {"ctx": z_cross, "tp": z}]
    for partner in partners:
        pl.semaphore_signal(barrier, inc=1, device_id=partner, device_id_type=MESH)

    local = [
        pltpu.make_async_copy(q_ref, qbuf.at[0, 0], local_sem.at[0]),
        pltpu.make_async_copy(sk_ref, skbuf, local_sem.at[1]),
        pltpu.make_async_copy(nk_ref, nkbuf, local_sem.at[2]),
        pltpu.make_async_copy(nv_ref, nvbuf, local_sem.at[3]),
        pltpu.make_async_copy(sv_ref, svbuf, local_sem.at[4]),
        pltpu.make_async_copy(k_ref, kbuf.at[0], local_sem.at[5]),
        pltpu.make_async_copy(v_ref, vbuf.at[0, :, 0:head_dim], local_sem.at[6]),
        pltpu.make_async_copy(w_ref, wbuf.at[0], local_sem.at[7]),
    ]
    for copy in local:
        copy.start()
    for c in range(CORES):
        vbuf[c, :, head_dim:] = jnp.ones((keys, LANES), jnp.bfloat16)

    pl.semaphore_wait(barrier, len(partners))
    local[0].wait()
    lines = []
    for k in range(ny // 2):
        first = 1 + (k + 2) % (ny // 2)
        lines += [first, (ny - first) * (1 - first // (ny // 2))]
    for dy in lines:
        for dx in far_first:
            if dx or dy:
                q_copy(dx, dy).start()
    k_core().start()
    v_core().start()

    for copy in local[1:5]:
        copy.wait()
    own_queries = qbuf[0, 0]
    row_in_sample = lax.broadcasted_iota(jnp.int32, (samp_rows, 1), 0)
    slot_index = lax.broadcasted_iota(jnp.int32, (samp_rows, slots), 1)
    tops = []
    for s in range(samp_dev):
        queries = own_queries[s * samp_rows : (s + 1) * samp_rows]
        scores = dot_rows(queries, skbuf[s])
        scores = jnp.where(slot_index < len_ref[s], scores, masked_score)
        new_keys = nkbuf[s].astype(jnp.float32)
        new_values = nvbuf[s].astype(jnp.float32)
        row_top = jnp.max(scores, axis=1, keepdims=True)
        recent = []
        for u in range(steps):
            score = jnp.sum(
                queries.astype(jnp.float32) * new_keys[u : u + 1], axis=1, keepdims=True
            )
            score = jnp.where(row_in_sample >= u * heads, score, masked_score)
            row_top = jnp.maximum(row_top, score)
            recent.append(score)
        weights = jnp.exp2((scores - row_top) * log2_scale)
        row_total = jnp.sum(weights, axis=1, keepdims=True)
        weighted = dot(weights.astype(jnp.bfloat16), svbuf[s])
        for u in range(steps):
            weight = jnp.exp2((recent[u] - row_top) * log2_scale)
            row_total = row_total + weight
            weighted = weighted + weight.astype(jnp.bfloat16).astype(jnp.float32) * (
                new_values[u : u + 1]
            )
        suffix_part[s * samp_rows : (s + 1) * samp_rows, :] = weighted / row_total
        tops.append(row_top * log2_scale + jnp.log2(row_total))
    lane = lax.broadcasted_iota(jnp.int32, (rows, LANES), 1)
    sub = lax.broadcasted_iota(jnp.int32, (rows, LANES), 0)
    suffix_top[...] = jnp.sum(
        jnp.where(lax.rem(lane, rows) == sub, jnp.concatenate(tops, axis=0), 0.0),
        axis=0,
        keepdims=True,
    )

    local[5].wait()
    local[6].wait()
    k_core().wait_recv()
    v_core().wait_recv()
    w_core().start()

    eye = lax.broadcasted_iota(jnp.int32, (LANES, LANES), 0) == lax.broadcasted_iota(
        jnp.int32, (LANES, LANES), 1
    )
    width = min(keys, 256)

    def attend(queries):
        row_top = weighted = None
        for c in range(CORES):
            for start in range(0, keys, width):
                scores = dot_rows(queries, kbuf[c, start : start + width])
                block_top = jnp.max(scores, axis=1, keepdims=True)
                top = block_top if row_top is None else jnp.maximum(row_top, block_top)
                weights = jnp.exp2((scores - top) * log2_scale).astype(jnp.bfloat16)
                term = dot(weights, vbuf[c, start : start + width])
                if row_top is not None:
                    term = weighted * jnp.exp2((row_top - top) * log2_scale) + term
                row_top, weighted = top, term
        total = weighted[:, head_dim:]
        part = (weighted[:, :head_dim] / total).astype(jnp.bfloat16)
        return part, row_top * log2_scale + jnp.log2(total)

    def line_arrived(dy):
        return remote(qbuf.at[dy], qbuf.at[dy], send_sem.at[0], q_sem.at[dy], sibling)

    half = ny // 2

    def four(k, carry):
        pairs = []
        for i in range(2):
            first = 1 + lax.rem(2 * k + i + 2, half)
            pairs.append((first, (ny - first) * (1 - lax.div(first, half))))
        for first, second in pairs:
            line_arrived(first).wait_recv()

            @pl.when(second != 0)
            def _():
                line_arrived(second).wait_recv()

            @pl.when(second == 0)
            def _():
                mine = qbuf.at[0, 1:nx]
                remote(mine, mine, send_sem.at[0], q_sem.at[0], sibling).wait_recv()

        lines = [slot for both in pairs for slot in both]
        queries = jnp.concatenate(
            [qbuf[slot].reshape(line, head_dim) for slot in lines], axis=0
        )
        part, top = attend(queries)
        for i, slot in enumerate(lines):
            parts[slot] = part[i * line : (i + 1) * line].reshape(nx, rows, head_dim)
            part_tops[slot] = jnp.sum(
                jnp.where(eye, top[i * line : (i + 1) * line], 0.0), axis=0, keepdims=True
            )
        for first, second in pairs[::-1]:
            for dx in far_first:
                p_copy(dx, first).start()
                pt_copy(dx, first).start()

            @pl.when(second != 0)
            def _():
                for dx in far_first:
                    p_copy(dx, second).start()
                    pt_copy(dx, second).start()

            @pl.when(second == 0)
            def _():
                for dx in far_first:
                    if dx:
                        for copy in own_line_copy(dx):
                            copy.start()

        return carry

    lax.fori_loop(0, ny // 4, four, 0)

    got[0, 0] = parts[0, 0]
    got_tops[0, 0] = part_tops[0]
    arrivals = (
        (got.at[1:ny], *family(5)),
        (got_tops.at[1:ny], *family(6)),
        (got.at[0, 1:nx], *family(7)),
        (got_tops.at[0, 1:nx], *family(8)),
    )
    for ref, send, recv in arrivals:
        remote(ref, ref, send, recv, sibling).wait_recv()

    lane_row = lax.broadcasted_iota(jnp.int32, (1, LANES), 1)
    stats = []
    for dy in range(ny):
        flat = got_tops[dy, 0]
        for dx in range(1, nx):
            flat = jnp.where(lax.div(lane_row, rows) == dx, got_tops[dy, dx], flat)
        stats.append(flat)

    def over_groups(result, op):
        turn = LANES // 2
        while turn >= rows:
            result = op(result, pltpu.roll(result, turn, 1))
            turn //= 2
        return result

    own_top = suffix_top[...]
    row_top = jnp.maximum(
        over_groups(functools.reduce(jnp.maximum, stats), jnp.maximum), own_top
    )
    stats = [jnp.exp2(flat - row_top) for flat in stats]
    own_weight = jnp.exp2(own_top - row_top)
    inverse = 1.0 / (over_groups(functools.reduce(jnp.add, stats), jnp.add) + own_weight)
    own_column = jnp.sum(
        jnp.where(lane == sub, own_weight * inverse, 0.0), axis=1, keepdims=True
    )
    result = own_column * suffix_part[...]
    for dy in range(ny):
        spread = jnp.where(lax.rem(lane, rows) == sub, stats[dy] * inverse, 0.0)
        result = result + dot(spread.astype(jnp.bfloat16), got[dy].reshape(line, head_dim))
    abuf[0, 0] = result.astype(jnp.bfloat16)

    for d in order:
        a_y(d).start()
    for d in far_first:
        if d:
            a_x(d, 0).start()
    w_core().wait_recv()
    local[7].wait()
    for dy in reversed(order):
        a_y(dy).wait_recv()
        for d in far_first:
            if d:
                a_x(d, dy).start()

    share = ny * tokens * nx // nz

    def project(dx):
        for d in range(ny):
            place = pl.multiple_of(lax.rem(y0 - d + ny, ny) * rows, rows)
            attention32[dx, pl.ds(place, rows), :] = abuf[dx, d].astype(jnp.float32)
        features = jnp.concatenate(
            [
                attention32[dx, pl.ds(h, ny * tokens, stride=heads), :].astype(jnp.bfloat16)
                for h in range(heads)
            ],
            axis=1,
        )
        for cross in range(CORES):
            terms = dot(features, wbuf[cross]).astype(jnp.bfloat16)
            for j in range(nz // nx):
                z_send[dx, j, cross] = terms[j * share : (j + 1) * share]
        for j in range(nz // nx):
            z, copy = z_copy(dx, j, 0)
            z_copy(dx, j, 1)[1].start()

            @pl.when(z != z0)
            def _():
                copy.start()

            @pl.when(z == z0)
            def _():
                z_parts[z0 * CORES + c0] = z_send[dx, j, 0]

    project(0)
    for dx in sorted(range(1, nx), key=lambda d: min(d, nx - d)):
        came = abuf.at[dx]
        remote(came, came, send_sem.at[10], recv_sem.at[11 + dx], sibling).wait_recv()
        project(dx)

    sources = nz * CORES
    remote(z_parts.at[1:sources], z_parts.at[1:sources], *family(11), sibling).wait_recv()
    total = []
    for c in range(CORES):
        terms = z_parts[c].astype(jnp.float32)
        for z in range(1, nz):
            terms = terms + z_parts[z * CORES + c].astype(jnp.float32)
        total.append(terms.astype(jnp.bfloat16))
    row_out = lax.broadcasted_iota(jnp.int32, (CORES * share, CORES * share), 0)
    row_in = lax.broadcasted_iota(jnp.int32, (CORES * share, CORES * share), 1)
    core = lax.rem(lax.div(row_out, tokens), CORES)
    source = (
        core * share + lax.div(row_out, CORES * tokens) * tokens + lax.rem(row_out, tokens)
    )
    reorder = jnp.where(row_in == source, 1.0, 0.0).astype(jnp.bfloat16)
    out_ref[...] = dot(reorder, jnp.concatenate(total, axis=0)).astype(jnp.bfloat16)

    sent = qbuf.at[1:ny]
    remote(sent, sent, send_sem.at[0], q_sem.at[1], sibling).wait_send()
    sent = qbuf.at[0, 1:nx]
    remote(sent, sent, send_sem.at[0], q_sem.at[0], sibling).wait_send()
    for copy in (k_core, v_core, w_core):
        copy().wait_send()
    for ref, send, recv in arrivals:
        remote(ref, ref, send, recv, sibling).wait_send()
    remote(abuf.at[0, 1:ny], abuf.at[0, 1:ny], send_sem.at[9], a_sem.at[0], sibling).wait_send()
    remote(abuf.at[1:nx], abuf.at[1:nx], send_sem.at[10], recv_sem.at[10], sibling).wait_send()
    remote(z_parts.at[1:sources], z_parts.at[1:sources], *family(11), sibling).wait_send()


def per_device(
    sizes,
    queries,
    prefix_keys,
    prefix_values,
    suffix_keys,
    suffix_values,
    new_keys,
    new_values,
    suffix_lengths,
    out_weight,
):
    nx, ny, nz = sizes
    samp_dev, steps, heads, head_dim = queries.shape
    rows = samp_dev * steps * heads
    tokens = samp_dev * steps
    keys = prefix_keys.shape[0]
    slots = suffix_keys.shape[1]
    columns = out_weight.shape[1]
    share = ny * tokens * nx // nz
    bf16, f32 = jnp.bfloat16, jnp.float32
    anywhere = pl.BlockSpec(memory_space=pl.ANY)
    out = pl.pallas_call(
        functools.partial(attend_kernel, sizes),
        out_shape=jax.ShapeDtypeStruct((CORES * share, columns), bf16),
        in_specs=[anywhere] * 7 + [pl.BlockSpec(memory_space=pltpu.SMEM), anywhere],
        out_specs=pl.BlockSpec(memory_space=pltpu.VMEM),
        scratch_shapes=[
            pltpu.VMEM((CORES, keys, head_dim), bf16),
            pltpu.VMEM((CORES, keys, head_dim + LANES), bf16),
            pltpu.VMEM((samp_dev, slots, head_dim), bf16),
            pltpu.VMEM((samp_dev, slots, head_dim), bf16),
            pltpu.VMEM((samp_dev, steps, head_dim), bf16),
            pltpu.VMEM((samp_dev, steps, head_dim), bf16),
            pltpu.VMEM((CORES, heads * head_dim, columns), bf16),
            pltpu.VMEM((ny, nx, rows, head_dim), bf16),
            pltpu.VMEM((ny, nx, rows, head_dim), bf16),
            pltpu.VMEM((ny, 1, LANES), f32),
            pltpu.VMEM((ny, nx, rows, head_dim), bf16),
            pltpu.VMEM((ny, nx, 1, LANES), f32),
            pltpu.VMEM((rows, head_dim), f32),
            pltpu.VMEM((1, LANES), f32),
            pltpu.VMEM((nx, ny, rows, head_dim), bf16),
            pltpu.VMEM((nx, ny * rows, head_dim), f32),
            pltpu.VMEM((nx, nz // nx, CORES, share, columns), bf16),
            pltpu.VMEM((nz * CORES, share, columns), bf16),
            pltpu.SemaphoreType.DMA((8,)),
            pltpu.SemaphoreType.DMA((12,)),
            pltpu.SemaphoreType.DMA((11 + nx,)),
            pltpu.SemaphoreType.DMA((ny,)),
            pltpu.SemaphoreType.DMA((ny,)),
        ],
        compiler_params=pltpu.CompilerParams(
            collective_id=0, has_side_effects=True, vmem_limit_bytes=60 * 1024 * 1024
        ),
    )(
        queries.reshape(rows, head_dim),
        prefix_keys.reshape(keys, head_dim),
        prefix_values.reshape(keys, head_dim),
        suffix_keys.reshape(samp_dev, slots, head_dim),
        suffix_values.reshape(samp_dev, slots, head_dim),
        new_keys.reshape(samp_dev, steps, head_dim),
        new_values.reshape(samp_dev, steps, head_dim),
        suffix_lengths,
        out_weight,
    )
    return out.reshape(CORES * share // steps, steps, columns)


def solution(mesh, sizes=(4, 8, 8)):
    placed = (
        P("ctx", None, "tp", None),
        P("ctx", "tp", None),
        P("ctx", "tp", None),
        P("ctx", None, "tp", None),
        P("ctx", None, "tp", None),
        P("ctx", None, "tp", None),
        P("ctx", None, "tp", None),
        P("ctx"),
        P("tp", "ctx"),
    )
    return jax.shard_map(
        functools.partial(per_device, sizes),
        mesh=mesh,
        in_specs=placed,
        out_specs=P("tp", None, "ctx"),
        check_vma=False,
    )
```
